512 devices in a mesh: cfg: 2 (over y_hi), seq: 32 (over z, y_lo), blk: 8 (over x, core).
Axes of the slice: x: 4, y: 8 (y_hi: 2, y_lo: 4; y = y_hi * 4 + y_lo), z: 8, core: 2. Of those that a mesh axis runs over, the one named last changes fastest.
Arguments:
- tokens_in: bfloat16 [2, 4096, 1536], P('cfg', 'seq'), may hold values from -6 to 6
- modulation: float32 [2, 8, 1536], replicated, may hold values from -3 to 3
- qk_gain: float32 [2, 64], replicated, as said below
- qkv_weight: bfloat16 [3, 1536, 1536], P(None, 'blk'), may hold values from -0.15625 to 0.15625
- out_weight: bfloat16 [1536, 1536], P('blk'), may hold values from -0.15625 to 0.15625
- up_weight: bfloat16 [1536, 6144], P('seq', 'blk'), may hold values from -0.15625 to 0.15625
- down_weight: bfloat16 [6144, 1536], P('blk', 'seq'), may hold values from -0.078125 to 0.078125
- proj_weight: bfloat16 [1536, 64], replicated, may hold values from -0.15625 to 0.15625
- latent: float32 [4096, 64], P(('seq', 'blk'), 'cfg'), may hold values from -6 to 6
- text_count: int32 [1], replicated, may hold values from 64 to 2047
- positions: int32 [3, 4096], P(None, 'seq'), may hold values from 0 to 47
- step_index: int32 [1], replicated, may hold values from 20 to 999
- guidance: float32 [1], replicated, may hold values from 4 to 8
Outputs:
- hidden_out: bfloat16 [2, 4096, 1536], P('cfg', ('seq', 'blk'))
- latent_prev: float32 [4096, 64], P(('seq', 'blk'), 'cfg')
The draws below stay inside these ranges and needn't reach their ends.
Inputs may be any that keep to these rules, and one draw needn't show every extreme that they name: `qk_gain`: positive gains.
All inputs are finite; a program needn't handle non-finite values.
Results may differ from the reference program's by a relative error of at most 0.015.
The reference program's roundings to bfloat16 on the way count: a program that leaves them out, or rounds other values in their place, can miss the bound.
Values may be sent and summed in bfloat16 or wider, within the bound.
No kernel may reach another device: no remote copies, remote signals or barrier semaphores. Data moves between devices by JAX's collectives and lax.ppermute only.
A program may use at most 64 MiB of HBM per device.

```python
import math
import jax
import jax.numpy as jnp
from jax import lax

D = 1536
HEADS = 24
HEAD = 64
FF = 6144
CH = 64
STRIDE = 20
TOK = 128
S = 4096


def draw_qk_gain(key, part):
    magnitude = jnp.exp(jax.random.uniform(key, (2, HEAD), jnp.float32, math.log(1.2), math.log(2.5)))
    return magnitude


def place_ends(result, key, low, top_value):
    dims = result.shape
    index_at = [jax.random.randint(jax.random.fold_in(key, axis), (), 0, dims[axis]) for axis in range(len(dims))]
    result = result.at[tuple(index_at)].set(low)
    longest = dims.index(max(dims))
    index_at[longest] = (index_at[longest] + 1) % dims[longest]
    return result.at[tuple(index_at)].set(top_value)


def block_levels(key, extent, split, low, largest):
    level, own = 1.0, jax.random.fold_in(key, 6)
    for position, parts in split:
        draws = jnp.exp(jax.random.uniform(jax.random.fold_in(own, position), (parts,), jnp.float32, low / len(split), largest / len(split)))
        level = level * jnp.repeat(draws, extent[position] // parts).reshape([-1 if axis == position else 1 for axis in range(len(extent))])
    return level


def centred(key, shape, width, most, cuts=(), held_as=jnp.bfloat16):
    loudness = block_levels(key, shape, cuts, -0.22, 0.18) if cuts else 1.0
    result = jax.random.normal(key, shape, jnp.float32) * width * loudness
    return jnp.minimum(jnp.maximum(result, -most), most).astype(held_as)


def setup_inputs(seed: int = 0) -> dict:
    keys = jax.random.split(jax.random.key(seed), 14)
    return {
        "tokens_in": centred(keys[0], (2, S, D), 1.0, 6.0, ((0, 2), (1, 32))),
        "modulation": centred(keys[1], (2, 8, D), 0.5, 3.0, (), jnp.float32),
        "qk_gain": draw_qk_gain(jax.random.fold_in(keys[13], 71), 0),
        "qkv_weight": centred(keys[3], (3, HEADS * HEAD, D), D ** -0.5, 0.15625, ((1, 8),)),
        "out_weight": centred(keys[4], (HEADS * HEAD, D), (HEADS * HEAD) ** -0.5, 0.15625, ((0, 8),)),
        "up_weight": centred(keys[5], (D, FF), D ** -0.5, 0.15625, ((0, 32), (1, 8))),
        "down_weight": centred(keys[6], (FF, D), FF ** -0.5, 0.078125, ((0, 8), (1, 32))),
        "proj_weight": centred(keys[7], (D, CH), D ** -0.5, 0.15625),
        "latent": centred(keys[8], (S, CH), 1.0, 6.0, ((0, 256), (1, 2)), jnp.float32),
        "text_count": jax.random.randint(keys[9], (1,), TOK // 2, S // 2).astype(jnp.int32),
        "positions": place_ends(jax.random.randint(keys[10], (3, S), 0, 48), jax.random.fold_in(keys[10], 1), 0, 47).astype(jnp.int32),
        "step_index": jax.random.randint(keys[11], (1,), STRIDE, 1000).astype(jnp.int32),
        "guidance": jnp.clip(jax.random.uniform(keys[12], (1,), jnp.float32, 4.0, 8.0), 4.0, 8.0),
    }


rope_bands = (16, 24, 24)

def layer_norm(values, epsilon):
    average = lax.optimization_barrier(jnp.mean(values, -1, keepdims=True))
    centered = values - average
    spread = lax.optimization_barrier(jnp.mean(centered * centered, -1, keepdims=True))
    return centered * lax.rsqrt(spread + epsilon)

def pick_mods(modulation, is_video, which):
    return jnp.where(is_video[:, None], modulation[1, which][None, :], modulation[0, which][None, :])

def modulate(values, modulation, is_video, shift_row, scale_row):
    normed = layer_norm(values, 1e-05)
    return normed * (1.0 + pick_mods(modulation, is_video, scale_row)) + pick_mods(modulation, is_video, shift_row)

def rope_tables(positions, is_video):
    angle_parts = []
    for axis_pos, band_width in enumerate(rope_bands):
        exponent = jnp.arange(band_width // 2, dtype=jnp.float32) * (2.0 / band_width)
        inverse = jnp.exp(-exponent * math.log(10000.0))
        angle_parts.append(positions[axis_pos].astype(jnp.float32)[:, None] * inverse[None, :])
    angles = jnp.concatenate(angle_parts, 1) * is_video.astype(jnp.float32)[:, None]
    return (jnp.cos(angles), jnp.sin(angles))

def rotate(vectors, cosine, sine):
    pieces = []
    offset = 0
    half_offset = 0
    for band_width in rope_bands:
        half_width = band_width // 2
        first_half = vectors[..., offset:offset + half_width]
        second = vectors[..., offset + half_width:offset + band_width]
        cos_band = cosine[:, None, half_offset:half_offset + half_width]
        sin_band = sine[:, None, half_offset:half_offset + half_width]
        pieces.append(first_half * cos_band - second * sin_band)
        pieces.append(second * cos_band + first_half * sin_band)
        offset = offset + band_width
        half_offset = half_offset + half_width
    return jnp.concatenate(pieces, -1)

def head_prep(flat_heads, gain, cosine, sine):
    token_count = flat_heads.shape[0]
    shaped = flat_heads.reshape(token_count, -1, HEAD)
    normed = layer_norm(shaped, 1e-06) * gain[None, None, :]
    turned = rotate(normed, cosine, sine)
    return turned.reshape(token_count, -1).astype(jnp.bfloat16)

def ddim_update(latent, guided, step_index):
    steps_all = jnp.arange(1000, dtype=jnp.float32)
    root_beta = math.sqrt(0.00085) + steps_all / 999.0 * (math.sqrt(0.012) - math.sqrt(0.00085))
    alpha_bar = jnp.exp(jnp.cumsum(jnp.log1p(-root_beta * root_beta)))
    indices = jnp.arange(1000, dtype=jnp.int32)
    alpha_now = jnp.sum(jnp.where(indices == step_index[0], alpha_bar, 0.0))
    alpha_prev = jnp.sum(jnp.where(indices == step_index[0] - STRIDE, alpha_bar, 0.0))
    clean_est = jnp.sqrt(alpha_now) * latent - jnp.sqrt(1.0 - alpha_now) * guided
    noise_est = jnp.sqrt(1.0 - alpha_now) * latent + jnp.sqrt(alpha_now) * guided
    return jnp.sqrt(alpha_prev) * clean_est + jnp.sqrt(1.0 - alpha_prev) * noise_est

def attend_head(operands):
    query_head, key_head, value_head = operands
    scores = jnp.dot(query_head.astype(jnp.float32), key_head.astype(jnp.float32).T, precision=lax.Precision.HIGHEST) * 0.125
    row_max = lax.optimization_barrier(jnp.max(scores, -1, keepdims=True))
    expo = jnp.exp(scores - row_max)
    row_sum = lax.optimization_barrier(jnp.sum(expo, -1, keepdims=True))
    weighted = jnp.dot(expo.astype(jnp.bfloat16).astype(jnp.float32), value_head.astype(jnp.float32), precision=lax.Precision.HIGHEST)
    return weighted / row_sum

def run_branch(branch_in, modulation, qk_gain, qkv_weight, out_weight, up_weight, down_weight, proj_weight, is_video, cosine, sine):
    residual = branch_in.astype(jnp.float32)
    normed = modulate(residual, modulation, is_video, 0, 1).astype(jnp.bfloat16)
    projected = jnp.einsum('td,ked->kte', normed.astype(jnp.float32), qkv_weight.astype(jnp.float32), precision=lax.Precision.HIGHEST)
    queries = head_prep(projected[0], qk_gain[0], cosine, sine)
    keys_all = head_prep(projected[1], qk_gain[1], cosine, sine)
    values_all = projected[2].astype(jnp.bfloat16)
    query_heads = queries.reshape(S, HEADS, HEAD).transpose(1, 0, 2)
    key_heads = keys_all.reshape(S, HEADS, HEAD).transpose(1, 0, 2)
    value_heads = values_all.reshape(S, HEADS, HEAD).transpose(1, 0, 2)
    mixed = lax.map(attend_head, (query_heads, key_heads, value_heads))
    attn_out = mixed.transpose(1, 0, 2).reshape(S, HEADS * HEAD).astype(jnp.bfloat16)
    attn_proj = jnp.dot(attn_out, out_weight, preferred_element_type=jnp.float32)
    after_attn = residual + pick_mods(modulation, is_video, 2) * attn_proj
    normed_mlp = modulate(after_attn, modulation, is_video, 3, 4).astype(jnp.bfloat16)
    hidden_up = jnp.dot(normed_mlp, up_weight, preferred_element_type=jnp.float32)
    activated = jax.nn.gelu(hidden_up, approximate=True).astype(jnp.bfloat16)
    mlp_out = jnp.dot(activated, down_weight, preferred_element_type=jnp.float32)
    after_mlp = after_attn + pick_mods(modulation, is_video, 5) * mlp_out
    final_norm = modulate(after_mlp, modulation, is_video, 6, 7).astype(jnp.bfloat16)
    predicted = jnp.dot(final_norm, proj_weight, preferred_element_type=jnp.float32)
    return (after_mlp.astype(jnp.bfloat16), predicted)

def reference(tokens_in, modulation, qk_gain, qkv_weight, out_weight, up_weight, down_weight, proj_weight, latent, text_count, positions, step_index, guidance):
    token_ids = jnp.arange(S, dtype=jnp.int32)
    is_video = token_ids >= text_count[0]
    cosine, sine = rope_tables(positions, is_video)
    outputs = []
    predictions = []
    for branch in range(2):
        hidden, predicted = run_branch(tokens_in[branch], modulation, qk_gain, qkv_weight, out_weight, up_weight, down_weight, proj_weight, is_video, cosine, sine)
        outputs.append(hidden)
        predictions.append(predicted)
    guided = predictions[1] + guidance[0] * (predictions[0] - predictions[1])
    return (jnp.stack(outputs), ddim_update(latent, guided, step_index))
```

```python
import math

import jax
import jax.numpy as jnp
import numpy as np
from jax import lax
from jax.experimental import pallas as pl
from jax.experimental.pallas import tpu as pltpu
from jax.sharding import PartitionSpec as P

BF16 = jnp.bfloat16
F32 = jnp.float32
STRIDE = 20
TOK = 128
OWN = 16
D = 1536
UNITS = 768
SEQ = 32
BLK = 8
PIECE = 48

ALONG_Z = [[4 * z + y for z in range(8)] for y in range(4)]
ALONG_Y = [[4 * z + y for y in range(4)] for z in range(8)]

VMEM = pl.BlockSpec(memory_space=pltpu.VMEM)
SMEM = pl.BlockSpec(memory_space=pltpu.SMEM)
ANY = pl.BlockSpec(memory_space=pl.ANY)

ROWS_BY_ROWS = (((1,), (1,)), ((), ()))


def frequencies():
    table = np.zeros((8, 128), np.float32)
    offset = 0
    for band, width in enumerate((16, 24, 24)):
        half = width // 2
        inverse = np.exp(-np.arange(half, dtype=np.float32) * np.float32(2.0 / width) * np.float32(math.log(10000.0)))
        for head in (0, 64):
            start = head + offset
            table[0, start : start + half] = inverse
            table[0, start + half : start + width] = inverse
            table[1, start : start + width] = band
            table[2, start : start + half] = 1.0
        offset += width
    return table


def layer_norm(values, epsilon):
    centered = values - jnp.mean(values, -1, keepdims=True)
    spread = jnp.mean(centered * centered, -1, keepdims=True)
    return centered * lax.rsqrt(spread + epsilon)


def picker(mods, video):
    return lambda row: jnp.where(video, mods[1, row : row + 1, :], mods[0, row : row + 1, :])


def project_kernel(where, text, tokens, mods, gain, qkv, positions, table, out):
    ids = where[1] * TOK + lax.broadcasted_iota(jnp.int32, (TOK, 1), 0)
    video = ids >= text[0]
    pick = picker(mods, video)
    residual = tokens[0].astype(F32)
    normed = (layer_norm(residual, 1e-05) * (1.0 + pick(1)) + pick(0)).astype(BF16)

    def project(weight):
        return lax.dot_general(normed, weight, ROWS_BY_ROWS, preferred_element_type=F32)

    heads = project(qkv[0:2].reshape(384, D))
    values_low = project(qkv[2, 0:128, :])
    values_high = project(qkv[2, 64:192, :])

    lane = lax.broadcasted_iota(jnp.int32, (TOK, 128), 1)
    low = lane < 64
    band = table[1:2, :]
    where_at = positions[...].astype(F32)
    spread = [jnp.broadcast_to(where_at[a : a + 1, :], (128, 128)).T for a in range(3)]
    chosen = jnp.where(band == 0.0, spread[0], jnp.where(band == 1.0, spread[1], spread[2]))
    angles = chosen * table[0:1, :] * video.astype(F32)
    cosine = jnp.cos(angles)
    sine = jnp.sin(angles)
    first = table[2:3, :] > 0.5
    sine = jnp.where(first, -sine, sine)
    narrow = band == 0.0

    row_head = lax.broadcasted_iota(jnp.int32, (128, 128), 0) >> 6
    average = jnp.where(row_head == (lane >> 6), 1.0 / 64.0, 0.0)

    def head_mean(block):
        return jnp.dot(block, average, precision=lax.Precision.HIGHEST, preferred_element_type=F32)

    def prepare(block, gains):
        centered = block - head_mean(block)
        normal = centered * lax.rsqrt(head_mean(centered * centered) + 1e-06) * gains
        ahead = jnp.where(narrow, pltpu.roll(normal, 120, 1), pltpu.roll(normal, 116, 1))
        behind = jnp.where(narrow, pltpu.roll(normal, 8, 1), pltpu.roll(normal, 12, 1))
        return normal * cosine + jnp.where(first, ahead, behind) * sine

    query_gain = jnp.concatenate([gain[0:1, :], gain[0:1, :]], 1)
    key_gain = jnp.concatenate([gain[1:2, :], gain[1:2, :]], 1)
    mixed_gain = jnp.concatenate([gain[0:1, :], gain[1:2, :]], 1)
    queries_low = prepare(heads[:, 0:128], query_gain)
    query_and_key = prepare(heads[:, 128:256], mixed_gain)
    keys_high = prepare(heads[:, 256:384], key_gain)

    def turned(block):
        return pltpu.roll(block, 64, 1)

    pairs = [
        jnp.where(low, turned(query_and_key), turned(values_low)),
        jnp.where(low, keys_high, values_low),
        jnp.where(low, turned(keys_high), values_high),
    ]
    queries = [
        (queries_low, turned(queries_low)),
        (turned(queries_low), queries_low),
        (query_and_key, turned(query_and_key)),
    ]
    low16 = low[0:16, :]
    for head in range(3):
        pair = pairs[head].astype(BF16)
        left, right = queries[head]
        for part in range(4):
            start = 32 * part
            packed = jnp.where(low16, left[start : start + 16, :], right[start + 16 : start + 32, :])
            packed = (packed * 0.125).astype(BF16)
            for half in range(2):
                goes = 8 * head + 4 * half + part
                out[goes, 0:64, :] = pair[64 * half : 64 * half + 64, :]
                out[goes, 64:80, :] = packed
    out[24:32] = jnp.zeros((8, 80, 128), BF16)


def attend_kernel(got, out):
    pairs = got[:, 0:64, :].reshape(2048, 128)
    queries = got[:, 64:80, :].reshape(512, 128).astype(F32)
    lane = lax.broadcasted_iota(jnp.int32, (256, 128), 1)
    low = lane < 64
    for side in range(2):
        turned = queries if side == 0 else pltpu.roll(queries, 64, 1)
        for chunk in range(2):
            block = jnp.where(low, turned[256 * chunk : 256 * chunk + 256, :], 0.0).astype(BF16)
            scores = lax.dot_general(block, pairs, ROWS_BY_ROWS, preferred_element_type=F32)
            highest = jnp.max(scores, -1, keepdims=True)
            weights = jnp.exp(scores - highest)
            total = jnp.sum(weights, -1, keepdims=True)
            mixed = jnp.dot(weights.astype(BF16), pairs, preferred_element_type=F32) / total
            level = highest + jnp.log(total)
            coarse = level.astype(BF16).astype(F32)
            medium = (level - coarse).astype(BF16).astype(F32)
            fine = level - coarse - medium
            parts = jnp.where(lane == 0, coarse, jnp.where(lane == 1, medium, fine))
            result = jnp.where(low, parts, mixed).astype(BF16)
            out[16 * chunk : 16 * chunk + 16, 16 * side : 16 * side + 16, :] = result.reshape(16, 16, 128)


def out_project_kernel(got, weight, out):
    total = None
    for head in range(3):
        sides = []
        for half in range(2):
            first = 8 * head + 4 * half
            block = got[first : first + 4].reshape(TOK, 128).astype(F32)
            level = block[:, 0:1] + block[:, 1:2] + block[:, 2:3]
            sides.append((block, level))
        (one, level_one), (two, level_two) = sides
        highest = jnp.maximum(level_one, level_two)
        share_one = jnp.exp(level_one - highest)
        share_two = jnp.exp(level_two - highest)
        mixed = (one * share_one + two * share_two) / (share_one + share_two)
        attended = mixed[:, 64:128].astype(BF16)
        term = jnp.dot(attended, weight[64 * head : 64 * head + 64, :], preferred_element_type=F32)
        total = term if total is None else total + term
    out[...] = total.astype(BF16).reshape(BLK, OWN, D)


def own_video(where, text):
    ids = where[1] * TOK + where[2] * OWN + lax.broadcasted_iota(jnp.int32, (OWN, 1), 0)
    return ids >= text[0]


def sum_blocks(got):
    total = got[0].astype(F32)
    for block in range(1, BLK):
        total = total + got[block].astype(F32)
    return total


def after_attention_kernel(where, text, got, tokens, mods, after, out):
    pick = picker(mods, own_video(where, text))
    residual = tokens[0, pl.ds(pl.multiple_of(where[2] * OWN, OWN), OWN), :].astype(F32)
    summed = residual + pick(2) * sum_blocks(got)
    after[...] = summed
    normed = (layer_norm(summed, 1e-05) * (1.0 + pick(4)) + pick(3)).astype(BF16)
    for block in range(BLK):
        out[block] = normed


def feed_forward_kernel(rows, weights, out, up, down, up_arrived, down_arrived):
    up_copy = pltpu.make_async_copy(weights.at[:, 0:PIECE, :], up, up_arrived)
    down_copy = pltpu.make_async_copy(weights.at[:, PIECE : 2 * PIECE, :], down, down_arrived)
    up_copy.start()
    down_copy.start()
    block = rows[...].reshape(TOK, D)
    up_copy.wait()
    hidden = jnp.dot(block, up[...].reshape(D, UNITS), preferred_element_type=F32)
    activated = jax.nn.gelu(hidden, approximate=True).astype(BF16)
    down_copy.wait()
    result = lax.dot_general(activated, down[...].reshape(D, UNITS), ROWS_BY_ROWS, preferred_element_type=F32)
    out[...] = result.astype(BF16).reshape(BLK, OWN, D)


def predict_kernel(where, text, got, after, mods, weight, hidden_out, predicted):
    pick = picker(mods, own_video(where, text))
    after_mlp = after[...] + pick(5) * sum_blocks(got)
    hidden_out[0] = after_mlp.astype(BF16)
    normed = (layer_norm(after_mlp, 1e-05) * (1.0 + pick(7)) + pick(6)).astype(BF16)
    predicted[...] = jnp.dot(normed, weight[...], preferred_element_type=F32)


def step_kernel(where, step, guidance, mine, other, latent, out):
    row = lax.broadcasted_iota(jnp.int32, (8, 128), 0)
    steps = row * 128 + lax.broadcasted_iota(jnp.int32, (8, 128), 1)
    low, high = math.sqrt(0.00085), math.sqrt(0.012)
    root_beta = low + steps.astype(F32) / 999.0 * (high - low)
    logs = jnp.log1p(-jnp.where(steps < 1000, root_beta * root_beta, 0.0))

    def alpha_bar(last):
        kept = jnp.where(steps <= last, logs, 0.0)
        return jnp.exp(jnp.sum(jnp.sum(kept, 1, keepdims=True), 0, keepdims=True))

    alpha_now = alpha_bar(step[0])
    alpha_prev = alpha_bar(step[0] - STRIDE)
    is_cond = where[0] == 0
    own, partner = mine[...], other[...]
    cond = jnp.where(is_cond, own, partner)
    uncond = jnp.where(is_cond, partner, own)
    both = uncond + guidance[0] * (cond - uncond)
    guided = jnp.where(is_cond, both[:, 0:32], both[:, 32:64])
    held = latent[...]
    root_now, root_rest = jnp.sqrt(alpha_now), jnp.sqrt(1.0 - alpha_now)
    clean = root_now * held - root_rest * guided
    noise = root_rest * held + root_now * guided
    out[...] = jnp.sqrt(alpha_prev) * clean + jnp.sqrt(1.0 - alpha_prev) * noise


def call(kernel, specs, shapes, mib=24, flops=10_000_000, scratch=()):
    return pl.pallas_call(
        kernel,
        out_shape=shapes,
        in_specs=specs,
        out_specs=jax.tree.map(lambda _: VMEM, shapes),
        scratch_shapes=scratch,
        compiler_params=pltpu.CompilerParams(vmem_limit_bytes=mib * 2**20),
        cost_estimate=pl.CostEstimate(flops=flops, bytes_accessed=4_000_000, transcendentals=0),
    )


def body(
    tokens_in,
    modulation,
    qk_gain,
    qkv_weight,
    out_weight,
    up_weight,
    down_weight,
    proj_weight,
    latent,
    text_count,
    positions,
    step_index,
    guidance,
):
    where = jnp.stack([lax.axis_index("cfg"), lax.axis_index("seq"), lax.axis_index("blk")]).astype(jnp.int32)

    piece = jnp.concatenate([up_weight, down_weight.T], 0)
    pieces = jnp.broadcast_to(piece[None], (4, 2 * PIECE, UNITS))
    pieces = lax.all_to_all(pieces, "seq", 0, 0, tiled=True, axis_index_groups=ALONG_Y)
    weights = lax.all_gather(
        pieces.reshape(8 * PIECE, UNITS), "seq", axis=0, tiled=True, axis_index_groups=ALONG_Z
    ).reshape(SEQ, 2 * PIECE, UNITS)

    sent = call(
        project_kernel,
        [SMEM, SMEM, VMEM, VMEM, VMEM, VMEM, VMEM, VMEM],
        jax.ShapeDtypeStruct((SEQ, 80, 128), BF16),
    )(where, text_count, tokens_in, modulation, qk_gain, qkv_weight, positions, jnp.asarray(frequencies()))
    got = lax.all_to_all(sent, "seq", 0, 0, tiled=True)
    attended = call(attend_kernel, [VMEM], jax.ShapeDtypeStruct((SEQ, 32, 128), BF16))(got)
    back = lax.all_to_all(attended, "seq", 0, 0, tiled=True)
    blocks = jax.ShapeDtypeStruct((BLK, OWN, D), BF16)
    partial = call(out_project_kernel, [VMEM, VMEM], blocks)(back, out_weight)
    partial = lax.all_to_all(partial, "blk", 0, 0, tiled=True)
    after, rows = call(
        after_attention_kernel,
        [SMEM, SMEM, VMEM, VMEM, VMEM],
        (jax.ShapeDtypeStruct((OWN, D), F32), blocks),
    )(where, text_count, partial, tokens_in, modulation)
    rows = lax.all_to_all(rows, "blk", 0, 0, tiled=True)
    half_weight = pltpu.VMEM((SEQ, PIECE, UNITS), BF16)
    mlp = call(
        feed_forward_kernel,
        [VMEM, ANY],
        blocks,
        scratch=[half_weight, half_weight, pltpu.SemaphoreType.DMA, pltpu.SemaphoreType.DMA],
    )(rows, weights)
    mlp = lax.all_to_all(mlp, "blk", 0, 0, tiled=True)
    hidden_out, predicted = call(
        predict_kernel,
        [SMEM, SMEM, VMEM, VMEM, VMEM, VMEM],
        (jax.ShapeDtypeStruct((1, OWN, D), BF16), jax.ShapeDtypeStruct((OWN, 64), F32)),
    )(where, text_count, mlp, after, modulation, proj_weight)
    partner = lax.ppermute(predicted, "cfg", [(0, 1), (1, 0)])
    latent_prev = call(
        step_kernel,
        [SMEM, SMEM, SMEM, VMEM, VMEM, VMEM],
        jax.ShapeDtypeStruct((OWN, 32), F32),
    )(where, step_index, guidance, predicted, partner, latent)
    return (hidden_out, latent_prev)


def solution(mesh):
    in_specs = (
        P("cfg", "seq", None),
        P(),
        P(),
        P(None, "blk", None),
        P("blk", None),
        P("seq", "blk"),
        P("blk", "seq"),
        P(),
        P(("seq", "blk"), "cfg"),
        P(),
        P(None, "seq"),
        P(),
        P(),
    )
    out_specs = (P("cfg", ("seq", "blk"), None), P(("seq", "blk"), "cfg"))
    return jax.shard_map(body, mesh=mesh, in_specs=in_specs, out_specs=out_specs, check_vma=False)
```

```python
import math

import jax
import jax.numpy as jnp
import numpy as np
from jax import lax
from jax.experimental import pallas as pl
from jax.experimental.pallas import tpu as pltpu
from jax.sharding import PartitionSpec as P

BF16 = jnp.bfloat16
F32 = jnp.float32
STRIDE = 20
TOK = 128
OWN = 16
D = 1536
UNITS = 768
SEQ = 32
BLK = 8
PIECE = 48

ALONG_Y = [[4 * z + y for y in range(4)] for z in range(8)]

VMEM = pl.BlockSpec(memory_space=pltpu.VMEM)
SMEM = pl.BlockSpec(memory_space=pltpu.SMEM)
ANY = pl.BlockSpec(memory_space=pl.ANY)

ROWS_BY_ROWS = (((1,), (1,)), ((), ()))


def frequencies():
    table = np.zeros((8, 128), np.float32)
    offset = 0
    for band, width in enumerate((16, 24, 24)):
        half = width // 2
        inverse = np.exp(-np.arange(half, dtype=np.float32) * np.float32(2.0 / width) * np.float32(math.log(10000.0)))
        for head in (0, 64):
            start = head + offset
            table[0, start : start + half] = inverse
            table[0, start + half : start + width] = inverse
            table[1, start : start + width] = band
            table[2, start : start + half] = 1.0
        offset += width
    return table


def layer_norm(values, epsilon):
    centered = values - jnp.mean(values, -1, keepdims=True)
    spread = jnp.mean(centered * centered, -1, keepdims=True)
    return centered * lax.rsqrt(spread + epsilon)


def picker(mods, video):
    return lambda row: jnp.where(video, mods[1, row : row + 1, :], mods[0, row : row + 1, :])


def project_kernel(where, text, tokens_far, mods_far, gain, qkv_far, positions, table, out, tokens, mods, qkv, arrived):
    copies = [
        pltpu.make_async_copy(far, near, arrived.at[i])
        for i, (far, near) in enumerate(((tokens_far, tokens), (mods_far, mods), (qkv_far, qkv)))
    ]
    for copy in copies:
        copy.start()
    copies[0].wait()
    copies[1].wait()
    ids = where[1] * TOK + lax.broadcasted_iota(jnp.int32, (TOK, 1), 0)
    video = ids >= text[0]
    pick = picker(mods, video)
    residual = tokens[0].astype(F32)
    normed = (layer_norm(residual, 1e-05) * (1.0 + pick(1)) + pick(0)).astype(BF16)

    def project(weight):
        return lax.dot_general(normed, weight, ROWS_BY_ROWS, preferred_element_type=F32)

    copies[2].wait()
    heads = project(qkv[0:2].reshape(384, D))
    values_low = project(qkv[2, 0:128, :])
    values_high = project(qkv[2, 64:192, :])

    lane = lax.broadcasted_iota(jnp.int32, (TOK, 128), 1)
    low = lane < 64
    band = table[1:2, :]
    where_at = positions[...].astype(F32)
    spread = [jnp.broadcast_to(where_at[a : a + 1, :], (128, 128)).T for a in range(3)]
    chosen = jnp.where(band == 0.0, spread[0], jnp.where(band == 1.0, spread[1], spread[2]))
    angles = chosen * table[0:1, :] * video.astype(F32)
    cosine = jnp.cos(angles)
    sine = jnp.sin(angles)
    first = table[2:3, :] > 0.5
    sine = jnp.where(first, -sine, sine)
    narrow = band == 0.0

    row_head = lax.broadcasted_iota(jnp.int32, (128, 128), 0) >> 6
    average = jnp.where(row_head == (lane >> 6), 1.0 / 64.0, 0.0)

    def head_mean(block):
        return jnp.dot(block, average, precision=lax.Precision.HIGHEST, preferred_element_type=F32)

    def prepare(block, gains):
        centered = block - head_mean(block)
        normal = centered * lax.rsqrt(head_mean(centered * centered) + 1e-06) * gains
        ahead = jnp.where(narrow, pltpu.roll(normal, 120, 1), pltpu.roll(normal, 116, 1))
        behind = jnp.where(narrow, pltpu.roll(normal, 8, 1), pltpu.roll(normal, 12, 1))
        return normal * cosine + jnp.where(first, ahead, behind) * sine

    query_gain = jnp.concatenate([gain[0:1, :], gain[0:1, :]], 1)
    key_gain = jnp.concatenate([gain[1:2, :], gain[1:2, :]], 1)
    mixed_gain = jnp.concatenate([gain[0:1, :], gain[1:2, :]], 1)
    queries_low = prepare(heads[:, 0:128], query_gain)
    query_and_key = prepare(heads[:, 128:256], mixed_gain)
    keys_high = prepare(heads[:, 256:384], key_gain)

    def turned(block):
        return pltpu.roll(block, 64, 1)

    pairs = [
        jnp.where(low, turned(query_and_key), turned(values_low)),
        jnp.where(low, keys_high, values_low),
        jnp.where(low, turned(keys_high), values_high),
    ]
    queries = [
        (queries_low, turned(queries_low)),
        (turned(queries_low), queries_low),
        (query_and_key, turned(query_and_key)),
    ]
    low16 = low[0:16, :]
    for head in range(3):
        pair = pairs[head].astype(BF16)
        left, right = queries[head]
        for part in range(4):
            start = 32 * part
            packed = jnp.where(low16, left[start : start + 16, :], right[start + 16 : start + 32, :])
            packed = (packed * 0.125).astype(BF16)
            for half in range(2):
                goes = 8 * head + 4 * half + part
                out[goes, 0:64, :] = pair[64 * half : 64 * half + 64, :]
                out[goes, 64:80, :] = packed
    out[24:32] = jnp.zeros((8, 80, 128), BF16)


def attend_kernel(got, out):
    pairs = got[:, 0:64, :].reshape(2048, 128)
    queries = got[:, 64:80, :].reshape(512, 128).astype(F32)
    lane = lax.broadcasted_iota(jnp.int32, (256, 128), 1)
    low = lane < 64
    for side in range(2):
        turned = queries if side == 0 else pltpu.roll(queries, 64, 1)
        for chunk in range(2):
            block = jnp.where(low, turned[256 * chunk : 256 * chunk + 256, :], 0.0).astype(BF16)
            scores = lax.dot_general(block, pairs, ROWS_BY_ROWS, preferred_element_type=F32)
            highest = jnp.max(scores, -1, keepdims=True)
            weights = jnp.exp(scores - highest)
            total = jnp.sum(weights, -1, keepdims=True)
            mixed = jnp.dot(weights.astype(BF16), pairs, preferred_element_type=F32) / total
            level = highest + jnp.log(total)
            coarse = level.astype(BF16).astype(F32)
            medium = (level - coarse).astype(BF16).astype(F32)
            fine = level - coarse - medium
            parts = jnp.where(lane == 0, coarse, jnp.where(lane == 1, medium, fine))
            result = jnp.where(low, parts, mixed).astype(BF16)
            out[16 * chunk : 16 * chunk + 16, 16 * side : 16 * side + 16, :] = result.reshape(16, 16, 128)


def out_project_kernel(got, weight, out):
    total = None
    for head in range(3):
        sides = []
        for half in range(2):
            first = 8 * head + 4 * half
            block = got[first : first + 4].reshape(TOK, 128).astype(F32)
            level = block[:, 0:1] + block[:, 1:2] + block[:, 2:3]
            sides.append((block, level))
        (one, level_one), (two, level_two) = sides
        highest = jnp.maximum(level_one, level_two)
        share_one = jnp.exp(level_one - highest)
        share_two = jnp.exp(level_two - highest)
        mixed = (one * share_one + two * share_two) / (share_one + share_two)
        attended = mixed[:, 64:128].astype(BF16)
        term = jnp.dot(attended, weight[64 * head : 64 * head + 64, :], preferred_element_type=F32)
        total = term if total is None else total + term
    out[...] = total.astype(BF16).reshape(BLK, OWN, D)


def own_video(where, text):
    ids = where[1] * TOK + where[2] * OWN + lax.broadcasted_iota(jnp.int32, (OWN, 1), 0)
    return ids >= text[0]


def sum_blocks(got):
    total = got[0].astype(F32)
    for block in range(1, BLK):
        total = total + got[block].astype(F32)
    return total


def after_attention_kernel(where, text, got, tokens, mods, after, out):
    pick = picker(mods, own_video(where, text))
    residual = tokens[0, pl.ds(pl.multiple_of(where[2] * OWN, OWN), OWN), :].astype(F32)
    summed = residual + pick(2) * sum_blocks(got)
    after[...] = summed
    normed = (layer_norm(summed, 1e-05) * (1.0 + pick(4)) + pick(3)).astype(BF16)
    for block in range(BLK):
        out[block] = normed


def feed_forward_kernel(where, rows, *refs):
    weights, (out, up, down, arrived) = refs[:9], refs[9:]
    places = [(where[1] // 4 + 8 - away) % 8 * 4 for away in (0, 1, 2, 3, -1, -2, -3, 4, 4)]
    places[8] = places[8] + 2

    def copies(side, near):
        return [
            pltpu.make_async_copy(
                block.at[:, PIECE * side : PIECE * side + PIECE, :],
                near.at[pl.ds(place, block.shape[0])],
                arrived.at[side, i],
            )
            for i, (block, place) in enumerate(zip(weights, places))
        ]

    up_copies, down_copies = copies(0, up), copies(1, down)
    for copy in up_copies + down_copies:
        copy.start()
    block = rows[...].reshape(TOK, D)
    for copy in up_copies:
        copy.wait()
    hidden = jnp.dot(block, up[...].reshape(D, UNITS), preferred_element_type=F32)
    activated = jax.nn.gelu(hidden, approximate=True).astype(BF16)
    for copy in down_copies:
        copy.wait()
    result = lax.dot_general(activated, down[...].reshape(D, UNITS), ROWS_BY_ROWS, preferred_element_type=F32)
    out[...] = result.astype(BF16).reshape(BLK, OWN, D)


def predict_kernel(where, text, got, after, mods, weight, hidden_out, predicted):
    pick = picker(mods, own_video(where, text))
    after_mlp = after[...] + pick(5) * sum_blocks(got)
    hidden_out[0] = after_mlp.astype(BF16)
    normed = (layer_norm(after_mlp, 1e-05) * (1.0 + pick(7)) + pick(6)).astype(BF16)
    predicted[...] = jnp.dot(normed, weight[...], preferred_element_type=F32)


def step_kernel(where, step, guidance, mine, other, latent, out):
    row = lax.broadcasted_iota(jnp.int32, (8, 128), 0)
    steps = row * 128 + lax.broadcasted_iota(jnp.int32, (8, 128), 1)
    low, high = math.sqrt(0.00085), math.sqrt(0.012)
    root_beta = low + steps.astype(F32) / 999.0 * (high - low)
    logs = jnp.log1p(-jnp.where(steps < 1000, root_beta * root_beta, 0.0))

    def alpha_bar(last):
        kept = jnp.where(steps <= last, logs, 0.0)
        return jnp.exp(jnp.sum(jnp.sum(kept, 1, keepdims=True), 0, keepdims=True))

    alpha_now = alpha_bar(step[0])
    alpha_prev = alpha_bar(step[0] - STRIDE)
    is_cond = where[0] == 0
    own, partner = mine[...], other[...]
    cond = jnp.where(is_cond, own, partner)
    uncond = jnp.where(is_cond, partner, own)
    both = uncond + guidance[0] * (cond - uncond)
    guided = jnp.where(is_cond, both[:, 0:32], both[:, 32:64])
    held = latent[...]
    root_now, root_rest = jnp.sqrt(alpha_now), jnp.sqrt(1.0 - alpha_now)
    clean = root_now * held - root_rest * guided
    noise = root_rest * held + root_now * guided
    out[...] = jnp.sqrt(alpha_prev) * clean + jnp.sqrt(1.0 - alpha_prev) * noise


def call(kernel, specs, shapes, mib=24, flops=10_000_000, scratch=()):
    return pl.pallas_call(
        kernel,
        out_shape=shapes,
        in_specs=specs,
        out_specs=jax.tree.map(lambda _: VMEM, shapes),
        scratch_shapes=scratch,
        compiler_params=pltpu.CompilerParams(vmem_limit_bytes=mib * 2**20),
        cost_estimate=pl.CostEstimate(flops=flops, bytes_accessed=4_000_000, transcendentals=0),
    )


def body(
    tokens_in,
    modulation,
    qk_gain,
    qkv_weight,
    out_weight,
    up_weight,
    down_weight,
    proj_weight,
    latent,
    text_count,
    positions,
    step_index,
    guidance,
):
    where = jnp.stack([lax.axis_index("cfg"), lax.axis_index("seq"), lax.axis_index("blk")]).astype(jnp.int32)

    piece = jnp.concatenate([up_weight, down_weight.T], 0)
    pieces = jnp.broadcast_to(piece[None], (4, 2 * PIECE, UNITS))
    held = lax.all_to_all(pieces, "seq", 0, 0, tiled=True, axis_index_groups=ALONG_Y)

    def shifted(block, step):
        return lax.ppermute(block, "seq", [(s, (s + 4 * step) % SEQ) for s in range(SEQ)])

    sent = call(
        project_kernel,
        [SMEM, SMEM, ANY, ANY, VMEM, ANY, VMEM, VMEM],
        jax.ShapeDtypeStruct((SEQ, 80, 128), BF16),
        scratch=[
            pltpu.VMEM((1, TOK, D), BF16),
            pltpu.VMEM((2, 8, D), F32),
            pltpu.VMEM((3, 192, D), BF16),
            pltpu.SemaphoreType.DMA((3,)),
        ],
    )(where, text_count, tokens_in, modulation, qk_gain, qkv_weight, positions, jnp.asarray(frequencies()))
    sent, held = lax.optimization_barrier((sent, held))
    below, above = [shifted(held, 1)], [shifted(held, -1)]
    got = lax.all_to_all(sent, "seq", 0, 0, tiled=True)
    got, below, above = lax.optimization_barrier((got, below, above))
    attended = call(attend_kernel, [VMEM], jax.ShapeDtypeStruct((SEQ, 32, 128), BF16))(got)
    below.append(shifted(below[0], 1))
    above.append(shifted(above[0], -1))
    back = lax.all_to_all(attended, "seq", 0, 0, tiled=True)
    back, below, above = lax.optimization_barrier((back, below, above))
    blocks = jax.ShapeDtypeStruct((BLK, OWN, D), BF16)
    partial = call(out_project_kernel, [VMEM, VMEM], blocks)(back, out_weight)
    below.append(shifted(below[1], 1))
    above.append(shifted(above[1], -1))
    partial = lax.all_to_all(partial, "blk", 0, 0, tiled=True)
    partial, below, above = lax.optimization_barrier((partial, below, above))
    after, rows = call(
        after_attention_kernel,
        [SMEM, SMEM, VMEM, VMEM, VMEM],
        (jax.ShapeDtypeStruct((OWN, D), F32), blocks),
    )(where, text_count, partial, tokens_in, modulation)
    far_low = shifted(below[2][0:2], 1)
    far_high = shifted(above[2][2:4], -1)
    rows = lax.all_to_all(rows, "blk", 0, 0, tiled=True)
    half_weight = pltpu.VMEM((SEQ, PIECE, UNITS), BF16)
    weights = [held, *below, *above, far_low, far_high]
    mlp = call(
        feed_forward_kernel,
        [SMEM, VMEM] + [ANY] * len(weights),
        blocks,
        scratch=[half_weight, half_weight, pltpu.SemaphoreType.DMA((2, len(weights)))],
    )(where, rows, *weights)
    mlp = lax.all_to_all(mlp, "blk", 0, 0, tiled=True)
    hidden_out, predicted = call(
        predict_kernel,
        [SMEM, SMEM, VMEM, VMEM, VMEM, VMEM],
        (jax.ShapeDtypeStruct((1, OWN, D), BF16), jax.ShapeDtypeStruct((OWN, 64), F32)),
    )(where, text_count, mlp, after, modulation, proj_weight)
    partner = lax.ppermute(predicted, "cfg", [(0, 1), (1, 0)])
    latent_prev = call(
        step_kernel,
        [SMEM, SMEM, SMEM, VMEM, VMEM, VMEM],
        jax.ShapeDtypeStruct((OWN, 32), F32),
    )(where, step_index, guidance, predicted, partner, latent)
    return (hidden_out, latent_prev)


def solution(mesh):
    in_specs = (
        P("cfg", "seq", None),
        P(),
        P(),
        P(None, "blk", None),
        P("blk", None),
        P("seq", "blk"),
        P("blk", "seq"),
        P(),
        P(("seq", "blk"), "cfg"),
        P(),
        P(None, "seq"),
        P(),
        P(),
    )
    out_specs = (P("cfg", ("seq", "blk"), None), P(("seq", "blk"), "cfg"))
    return jax.shard_map(body, mesh=mesh, in_specs=in_specs, out_specs=out_specs, check_vma=False)
```

```python
import math

import jax
import jax.numpy as jnp
import numpy as np
from jax import lax
from jax.experimental import pallas as pl
from jax.experimental.pallas import tpu as pltpu
from jax.sharding import PartitionSpec as P

BF16 = jnp.bfloat16
F32 = jnp.float32
STRIDE = 20
TOK = 128
OWN = 16
D = 1536
UNITS = 384
SEQ = 32
BLK = 8
GROUP = 16
PIECE = 48

SEQ_AXES = ("z", "pair", "side")
LINE = ("pair", "side")
SHARERS = ("side", "blk")

VMEM = pl.BlockSpec(memory_space=pltpu.VMEM)
SMEM = pl.BlockSpec(memory_space=pltpu.SMEM)
ANY = pl.BlockSpec(memory_space=pl.ANY)
HBM = pl.BlockSpec(memory_space=pltpu.HBM)

ROWS_BY_ROWS = (((1,), (1,)), ((), ()))


def frequencies():
    table = np.zeros((8, 128), np.float32)
    offset = 0
    for band, width in enumerate((16, 24, 24)):
        half = width // 2
        inverse = np.exp(-np.arange(half, dtype=np.float32) * np.float32(2.0 / width) * np.float32(math.log(10000.0)))
        for head in (0, 64):
            start = head + offset
            table[0, start : start + half] = inverse
            table[0, start + half : start + width] = inverse
            table[1, start : start + width] = band
            table[2, start : start + half] = 1.0
        offset += width
    return table


def layer_norm(values, epsilon):
    centered = values - jnp.mean(values, -1, keepdims=True)
    spread = jnp.mean(centered * centered, -1, keepdims=True)
    return centered * lax.rsqrt(spread + epsilon)


def picker(mods, video):
    return lambda row: jnp.where(video, mods[1, row : row + 1, :], mods[0, row : row + 1, :])


def project_kernel(where, text, tokens_far, mods_far, gain, qkv_far, positions, table, out, tokens, mods, qkv, arrived):
    copies = [
        pltpu.make_async_copy(far, near, arrived.at[i])
        for i, (far, near) in enumerate(((tokens_far, tokens), (mods_far, mods), (qkv_far, qkv)))
    ]
    for copy in copies:
        copy.start()
    copies[0].wait()
    copies[1].wait()
    ids = where[1] * TOK + lax.broadcasted_iota(jnp.int32, (TOK, 1), 0)
    video = ids >= text[0]
    pick = picker(mods, video)
    residual = tokens[0].astype(F32)
    normed = (layer_norm(residual, 1e-05) * (1.0 + pick(1)) + pick(0)).astype(BF16)

    def project(weight):
        return lax.dot_general(normed, weight, ROWS_BY_ROWS, preferred_element_type=F32)

    copies[2].wait()
    heads = project(qkv[0:2].reshape(384, D))
    values_low = project(qkv[2, 0:128, :])
    values_high = project(qkv[2, 64:192, :])

    lane = lax.broadcasted_iota(jnp.int32, (TOK, 128), 1)
    low = lane < 64
    band = table[1:2, :]
    where_at = positions[...].astype(F32)
    spread = [jnp.broadcast_to(where_at[a : a + 1, :], (128, 128)).T for a in range(3)]
    chosen = jnp.where(band == 0.0, spread[0], jnp.where(band == 1.0, spread[1], spread[2]))
    angles = chosen * table[0:1, :] * video.astype(F32)
    cosine = jnp.cos(angles)
    sine = jnp.sin(angles)
    first = table[2:3, :] > 0.5
    sine = jnp.where(first, -sine, sine)
    narrow = band == 0.0

    row_head = lax.broadcasted_iota(jnp.int32, (128, 128), 0) >> 6
    average = jnp.where(row_head == (lane >> 6), 1.0 / 64.0, 0.0)

    def head_mean(block):
        return jnp.dot(block, average, precision=lax.Precision.HIGHEST, preferred_element_type=F32)

    def prepare(block, gains):
        centered = block - head_mean(block)
        normal = centered * lax.rsqrt(head_mean(centered * centered) + 1e-06) * gains
        ahead = jnp.where(narrow, pltpu.roll(normal, 120, 1), pltpu.roll(normal, 116, 1))
        behind = jnp.where(narrow, pltpu.roll(normal, 8, 1), pltpu.roll(normal, 12, 1))
        return normal * cosine + jnp.where(first, ahead, behind) * sine

    query_gain = jnp.concatenate([gain[0:1, :], gain[0:1, :]], 1)
    key_gain = jnp.concatenate([gain[1:2, :], gain[1:2, :]], 1)
    mixed_gain = jnp.concatenate([gain[0:1, :], gain[1:2, :]], 1)
    queries_low = prepare(heads[:, 0:128], query_gain)
    query_and_key = prepare(heads[:, 128:256], mixed_gain)
    keys_high = prepare(heads[:, 256:384], key_gain)

    def turned(block):
        return pltpu.roll(block, 64, 1)

    pairs = [
        jnp.where(low, turned(query_and_key), turned(values_low)),
        jnp.where(low, keys_high, values_low),
        jnp.where(low, turned(keys_high), values_high),
    ]
    queries = [
        (queries_low, turned(queries_low)),
        (turned(queries_low), queries_low),
        (query_and_key, turned(query_and_key)),
    ]
    low16 = low[0:16, :]
    for head in range(3):
        pair = pairs[head].astype(BF16)
        left, right = queries[head]
        for part in range(4):
            start = 32 * part
            packed = jnp.where(low16, left[start : start + 16, :], right[start + 16 : start + 32, :])
            packed = (packed * 0.125).astype(BF16)
            for half in range(2):
                goes = 8 * head + 4 * half + part
                out[goes, 0:64, :] = pair[64 * half : 64 * half + 64, :]
                out[goes, 64:80, :] = packed
    out[24:32] = jnp.zeros((8, 80, 128), BF16)


def attend_kernel(got, out):
    pairs = got[:, 0:64, :].reshape(2048, 128)
    queries = got[:, 64:80, :].reshape(512, 128).astype(F32)
    lane = lax.broadcasted_iota(jnp.int32, (256, 128), 1)
    low = lane < 64
    for side in range(2):
        turned = queries if side == 0 else pltpu.roll(queries, 64, 1)
        for chunk in range(2):
            block = jnp.where(low, turned[256 * chunk : 256 * chunk + 256, :], 0.0).astype(BF16)
            scores = lax.dot_general(block, pairs, ROWS_BY_ROWS, preferred_element_type=F32)
            highest = jnp.max(scores, -1, keepdims=True)
            weights = jnp.exp(scores - highest)
            total = jnp.sum(weights, -1, keepdims=True)
            mixed = jnp.dot(weights.astype(BF16), pairs, preferred_element_type=F32) / total
            level = highest + jnp.log(total)
            coarse = level.astype(BF16).astype(F32)
            medium = (level - coarse).astype(BF16).astype(F32)
            fine = level - coarse - medium
            parts = jnp.where(lane == 0, coarse, jnp.where(lane == 1, medium, fine))
            result = jnp.where(low, parts, mixed).astype(BF16)
            out[16 * chunk : 16 * chunk + 16, 16 * side : 16 * side + 16, :] = result.reshape(16, 16, 128)


def out_project_kernel(got, weight, out):
    total = None
    for head in range(3):
        sides = []
        for half in range(2):
            first = 8 * head + 4 * half
            block = got[first : first + 4].reshape(TOK, 128).astype(F32)
            level = block[:, 0:1] + block[:, 1:2] + block[:, 2:3]
            sides.append((block, level))
        (one, level_one), (two, level_two) = sides
        highest = jnp.maximum(level_one, level_two)
        share_one = jnp.exp(level_one - highest)
        share_two = jnp.exp(level_two - highest)
        mixed = (one * share_one + two * share_two) / (share_one + share_two)
        attended = mixed[:, 64:128].astype(BF16)
        term = jnp.dot(attended, weight[64 * head : 64 * head + 64, :], preferred_element_type=F32)
        total = term if total is None else total + term
    out[...] = total.astype(BF16).reshape(BLK, OWN, D)


def own_video(where, text):
    ids = where[1] * TOK + where[2] * OWN + lax.broadcasted_iota(jnp.int32, (OWN, 1), 0)
    return ids >= text[0]


def sum_blocks(got):
    total = got[0].astype(F32)
    for block in range(1, got.shape[0]):
        total = total + got[block].astype(F32)
    return total


def after_attention_kernel(where, text, got, tokens, mods, after, out):
    pick = picker(mods, own_video(where, text))
    residual = tokens[0, pl.ds(pl.multiple_of(where[2] * OWN, OWN), OWN), :].astype(F32)
    summed = residual + pick(2) * sum_blocks(got)
    after[...] = summed
    normed = (layer_norm(summed, 1e-05) * (1.0 + pick(4)) + pick(3)).astype(BF16)
    for block in range(GROUP):
        out[block] = normed


def feed_forward_kernel(rows, weights, out, up, down, up_arrived, down_arrived):
    up_copy = pltpu.make_async_copy(weights.at[:, 0:PIECE, :], up, up_arrived)
    down_copy = pltpu.make_async_copy(weights.at[:, PIECE : 2 * PIECE, :], down, down_arrived)
    up_copy.start()
    down_copy.start()
    block = rows[...].reshape(GROUP * OWN, D)
    up_copy.wait()
    hidden = jnp.dot(block, up[...].reshape(D, UNITS), preferred_element_type=F32)
    activated = jax.nn.gelu(hidden, approximate=True).astype(BF16)
    down_copy.wait()
    result = lax.dot_general(activated, down[...].reshape(D, UNITS), ROWS_BY_ROWS, preferred_element_type=F32)
    out[...] = result.astype(BF16).reshape(GROUP, OWN, D)


def pieces_kernel(up, down, out, arrived):
    copies = []
    for device in range(4):
        half = pl.ds(UNITS * (device % 2), UNITS)
        for side, weight in enumerate((up, down)):
            rows = pl.ds(PIECE * side, PIECE)
            copies.append(pltpu.make_async_copy(weight.at[:, half], out.at[device, rows, :], arrived.at[device, side]))
    for copy in copies:
        copy.start()
    for copy in copies:
        copy.wait()


def predict_kernel(where, text, got, after, mods, weight, hidden_out, predicted):
    pick = picker(mods, own_video(where, text))
    after_mlp = after[...] + pick(5) * sum_blocks(got)
    hidden_out[0] = after_mlp.astype(BF16)
    normed = (layer_norm(after_mlp, 1e-05) * (1.0 + pick(7)) + pick(6)).astype(BF16)
    predicted[...] = jnp.dot(normed, weight[...], preferred_element_type=F32)


def step_kernel(where, step, guidance, mine, other, latent, out):
    row = lax.broadcasted_iota(jnp.int32, (8, 128), 0)
    steps = row * 128 + lax.broadcasted_iota(jnp.int32, (8, 128), 1)
    low, high = math.sqrt(0.00085), math.sqrt(0.012)
    root_beta = low + steps.astype(F32) / 999.0 * (high - low)
    logs = jnp.log1p(-jnp.where(steps < 1000, root_beta * root_beta, 0.0))

    def alpha_bar(last):
        kept = jnp.where(steps <= last, logs, 0.0)
        return jnp.exp(jnp.sum(jnp.sum(kept, 1, keepdims=True), 0, keepdims=True))

    alpha_now = alpha_bar(step[0])
    alpha_prev = alpha_bar(step[0] - STRIDE)
    is_cond = where[0] == 0
    own, partner = mine[...], other[...]
    cond = jnp.where(is_cond, own, partner)
    uncond = jnp.where(is_cond, partner, own)
    both = uncond + guidance[0] * (cond - uncond)
    guided = jnp.where(is_cond, both[:, 0:32], both[:, 32:64])
    held = latent[...]
    root_now, root_rest = jnp.sqrt(alpha_now), jnp.sqrt(1.0 - alpha_now)
    clean = root_now * held - root_rest * guided
    noise = root_rest * held + root_now * guided
    out[...] = jnp.sqrt(alpha_prev) * clean + jnp.sqrt(1.0 - alpha_prev) * noise


def call(kernel, specs, shapes, mib=24, flops=10_000_000, scratch=()):
    return pl.pallas_call(
        kernel,
        out_shape=shapes,
        in_specs=specs,
        out_specs=jax.tree.map(lambda _: VMEM, shapes),
        scratch_shapes=scratch,
        compiler_params=pltpu.CompilerParams(vmem_limit_bytes=mib * 2**20),
        cost_estimate=pl.CostEstimate(flops=flops, bytes_accessed=4_000_000, transcendentals=0),
    )


def body(
    tokens_in,
    modulation,
    qk_gain,
    qkv_weight,
    out_weight,
    up_weight,
    down_weight,
    proj_weight,
    latent,
    text_count,
    positions,
    step_index,
    guidance,
):
    where = jnp.stack([lax.axis_index("cfg"), lax.axis_index(SEQ_AXES), lax.axis_index("blk")]).astype(jnp.int32)

    pieces = call(
        pieces_kernel,
        [HBM, HBM],
        jax.ShapeDtypeStruct((4, 2 * PIECE, UNITS), BF16),
        scratch=[pltpu.SemaphoreType.DMA((4, 2))],
    )(up_weight, down_weight.T)
    pieces = lax.all_to_all(pieces, LINE, 0, 0, tiled=True)

    sent = call(
        project_kernel,
        [SMEM, SMEM, ANY, ANY, VMEM, ANY, VMEM, VMEM],
        jax.ShapeDtypeStruct((SEQ, 80, 128), BF16),
        scratch=[
            pltpu.VMEM((1, TOK, D), BF16),
            pltpu.VMEM((2, 8, D), F32),
            pltpu.VMEM((3, 192, D), BF16),
            pltpu.SemaphoreType.DMA((3,)),
        ],
    )(where, text_count, tokens_in, modulation, qk_gain, qkv_weight, positions, jnp.asarray(frequencies()))
    sent, pieces = lax.optimization_barrier((sent, pieces))
    weights = lax.all_gather(pieces, "z", axis=0, tiled=True)
    got = lax.all_to_all(sent, SEQ_AXES, 0, 0, tiled=True)
    attended = call(attend_kernel, [VMEM], jax.ShapeDtypeStruct((SEQ, 32, 128), BF16))(got)
    back = lax.all_to_all(attended, SEQ_AXES, 0, 0, tiled=True)
    blocks = jax.ShapeDtypeStruct((BLK, OWN, D), BF16)
    shared = jax.ShapeDtypeStruct((GROUP, OWN, D), BF16)
    partial = call(out_project_kernel, [VMEM, VMEM], blocks)(back, out_weight)
    partial = lax.all_to_all(partial, "blk", 0, 0, tiled=True)
    after, rows = call(
        after_attention_kernel,
        [SMEM, SMEM, VMEM, VMEM, VMEM],
        (jax.ShapeDtypeStruct((OWN, D), F32), shared),
    )(where, text_count, partial, tokens_in, modulation)
    rows = lax.all_to_all(rows, SHARERS, 0, 0, tiled=True)
    half_weight = pltpu.VMEM((SEQ, PIECE, UNITS), BF16)
    mlp = call(
        feed_forward_kernel,
        [VMEM, HBM],
        shared,
        scratch=[half_weight, half_weight, pltpu.SemaphoreType.DMA, pltpu.SemaphoreType.DMA],
    )(rows, weights)
    mlp = lax.all_to_all(mlp, SHARERS, 0, 0, tiled=True)
    hidden_out, predicted = call(
        predict_kernel,
        [SMEM, SMEM, VMEM, VMEM, VMEM, VMEM],
        (jax.ShapeDtypeStruct((1, OWN, D), BF16), jax.ShapeDtypeStruct((OWN, 64), F32)),
    )(where, text_count, mlp, after, modulation, proj_weight)
    partner = lax.ppermute(predicted, "cfg", [(0, 1), (1, 0)])
    latent_prev = call(
        step_kernel,
        [SMEM, SMEM, SMEM, VMEM, VMEM, VMEM],
        jax.ShapeDtypeStruct((OWN, 32), F32),
    )(where, step_index, guidance, predicted, partner, latent)
    return (hidden_out, latent_prev)


def solution(mesh):
    devices = mesh.devices.reshape(2, 8, 2, 2, 8)
    fine = jax.sharding.Mesh(devices, ("cfg", *SEQ_AXES, "blk"))
    rows = (*SEQ_AXES, "blk")
    in_specs = (
        P("cfg", SEQ_AXES, None),
        P(),
        P(),
        P(None, "blk", None),
        P("blk", None),
        P(SEQ_AXES, "blk"),
        P("blk", SEQ_AXES),
        P(),
        P(rows, "cfg"),
        P(),
        P(None, SEQ_AXES),
        P(),
        P(),
    )
    out_specs = (P("cfg", rows, None), P(rows, "cfg"))
    return jax.shard_map(body, mesh=fine, in_specs=in_specs, out_specs=out_specs, check_vma=False)
```

```python
import math

import jax
import jax.numpy as jnp
import numpy as np
from jax import lax
from jax.experimental import pallas as pl
from jax.experimental.pallas import tpu as pltpu
from jax.sharding import PartitionSpec as P

BF16 = jnp.bfloat16
F32 = jnp.float32
STRIDE = 20
TOK = 128
OWN = 16
D = 1536
UNITS = 384
SEQ = 32
BLK = 8
GROUP = 8
PIECE = 48

SEQ_AXES = ("z", "pair", "side")
LINE = ("pair", "side")
BLK_AXES = ("x", "core")
SHARERS = ("side", "x")

VMEM = pl.BlockSpec(memory_space=pltpu.VMEM)
SMEM = pl.BlockSpec(memory_space=pltpu.SMEM)
ANY = pl.BlockSpec(memory_space=pl.ANY)
HBM = pl.BlockSpec(memory_space=pltpu.HBM)

ROWS_BY_ROWS = (((1,), (1,)), ((), ()))


def frequencies():
    table = np.zeros((8, 128), np.float32)
    offset = 0
    for band, width in enumerate((16, 24, 24)):
        half = width // 2
        inverse = np.exp(-np.arange(half, dtype=np.float32) * np.float32(2.0 / width) * np.float32(math.log(10000.0)))
        for head in (0, 64):
            start = head + offset
            table[0, start : start + half] = inverse
            table[0, start + half : start + width] = inverse
            table[1, start : start + width] = band
            table[2, start : start + half] = 1.0
        offset += width
    return table


def layer_norm(values, epsilon):
    centered = values - jnp.mean(values, -1, keepdims=True)
    spread = jnp.mean(centered * centered, -1, keepdims=True)
    return centered * lax.rsqrt(spread + epsilon)


def picker(mods, video):
    return lambda row: jnp.where(video, mods[1, row : row + 1, :], mods[0, row : row + 1, :])


def project_kernel(where, text, tokens_far, mods_far, gain_far, positions_far, table_far, qkv_far, out, *scratch):
    tokens, mods, gain, positions, table, qkv, arrived = scratch
    far = (tokens_far, mods_far, gain_far, positions_far, table_far, qkv_far)
    copies = [pltpu.make_async_copy(a, b, arrived.at[i]) for i, (a, b) in enumerate(zip(far, scratch))]
    for copy in copies:
        copy.start()
    for copy in copies[:5]:
        copy.wait()
    ids = where[1] * TOK + lax.broadcasted_iota(jnp.int32, (TOK, 1), 0)
    video = ids >= text[0]
    pick = picker(mods, video)
    residual = tokens[0].astype(F32)
    normed = (layer_norm(residual, 1e-05) * (1.0 + pick(1)) + pick(0)).astype(BF16)

    def project(weight):
        return lax.dot_general(normed, weight, ROWS_BY_ROWS, preferred_element_type=F32)

    copies[5].wait()
    heads = project(qkv[0:2].reshape(384, D))
    values_low = project(qkv[2, 0:128, :])
    values_high = project(qkv[2, 64:192, :])

    lane = lax.broadcasted_iota(jnp.int32, (TOK, 128), 1)
    low = lane < 64
    band = table[1:2, :]
    where_at = positions[...].astype(F32)
    spread = [jnp.broadcast_to(where_at[a : a + 1, :], (128, 128)).T for a in range(3)]
    chosen = jnp.where(band == 0.0, spread[0], jnp.where(band == 1.0, spread[1], spread[2]))
    angles = chosen * table[0:1, :] * video.astype(F32)
    cosine = jnp.cos(angles)
    sine = jnp.sin(angles)
    first = table[2:3, :] > 0.5
    sine = jnp.where(first, -sine, sine)
    narrow = band == 0.0

    row_head = lax.broadcasted_iota(jnp.int32, (128, 128), 0) >> 6
    average = jnp.where(row_head == (lane >> 6), 1.0 / 64.0, 0.0)

    def head_mean(block):
        return jnp.dot(block, average, precision=lax.Precision.HIGHEST, preferred_element_type=F32)

    def prepare(block, gains):
        centered = block - head_mean(block)
        normal = centered * lax.rsqrt(head_mean(centered * centered) + 1e-06) * gains
        ahead = jnp.where(narrow, pltpu.roll(normal, 120, 1), pltpu.roll(normal, 116, 1))
        behind = jnp.where(narrow, pltpu.roll(normal, 8, 1), pltpu.roll(normal, 12, 1))
        return normal * cosine + jnp.where(first, ahead, behind) * sine

    query_gain = jnp.concatenate([gain[0:1, :], gain[0:1, :]], 1)
    key_gain = jnp.concatenate([gain[1:2, :], gain[1:2, :]], 1)
    mixed_gain = jnp.concatenate([gain[0:1, :], gain[1:2, :]], 1)
    queries_low = prepare(heads[:, 0:128], query_gain)
    query_and_key = prepare(heads[:, 128:256], mixed_gain)
    keys_high = prepare(heads[:, 256:384], key_gain)

    def turned(block):
        return pltpu.roll(block, 64, 1)

    pairs = [
        jnp.where(low, turned(query_and_key), turned(values_low)),
        jnp.where(low, keys_high, values_low),
        jnp.where(low, turned(keys_high), values_high),
    ]
    queries = [
        (queries_low, turned(queries_low)),
        (turned(queries_low), queries_low),
        (query_and_key, turned(query_and_key)),
    ]
    low16 = low[0:16, :]
    for head in range(3):
        pair = pairs[head].astype(BF16)
        left, right = queries[head]
        for part in range(4):
            start = 32 * part
            packed = jnp.where(low16, left[start : start + 16, :], right[start + 16 : start + 32, :])
            packed = (packed * 0.125).astype(BF16)
            for half in range(2):
                goes = 8 * head + 4 * half + part
                out[goes, 0:64, :] = pair[64 * half : 64 * half + 64, :]
                out[goes, 64:80, :] = packed
    out[24:32] = jnp.zeros((8, 80, 128), BF16)


def attend_kernel(got, out):
    pairs = got[:, 0:64, :].reshape(2048, 128)
    queries = got[:, 64:80, :].reshape(512, 128).astype(F32)
    lane = lax.broadcasted_iota(jnp.int32, (256, 128), 1)
    low = lane < 64
    for side in range(2):
        turned = queries if side == 0 else pltpu.roll(queries, 64, 1)
        for chunk in range(2):
            block = jnp.where(low, turned[256 * chunk : 256 * chunk + 256, :], 0.0).astype(BF16)
            scores = lax.dot_general(block, pairs, ROWS_BY_ROWS, preferred_element_type=F32)
            highest = jnp.max(scores, -1, keepdims=True)
            weights = jnp.exp(scores - highest)
            total = jnp.sum(weights, -1, keepdims=True)
            mixed = jnp.dot(weights.astype(BF16), pairs, preferred_element_type=F32) / total
            level = highest + jnp.log(total)
            coarse = level.astype(BF16).astype(F32)
            medium = (level - coarse).astype(BF16).astype(F32)
            fine = level - coarse - medium
            parts = jnp.where(lane == 0, coarse, jnp.where(lane == 1, medium, fine))
            result = jnp.where(low, parts, mixed).astype(BF16)
            out[16 * chunk : 16 * chunk + 16, 16 * side : 16 * side + 16, :] = result.reshape(16, 16, 128)


def out_project_kernel(got, weight, out):
    total = None
    for head in range(3):
        sides = []
        for half in range(2):
            first = 8 * head + 4 * half
            block = got[first : first + 4].reshape(TOK, 128).astype(F32)
            level = block[:, 0:1] + block[:, 1:2] + block[:, 2:3]
            sides.append((block, level))
        (one, level_one), (two, level_two) = sides
        highest = jnp.maximum(level_one, level_two)
        share_one = jnp.exp(level_one - highest)
        share_two = jnp.exp(level_two - highest)
        mixed = (one * share_one + two * share_two) / (share_one + share_two)
        attended = mixed[:, 64:128].astype(BF16)
        term = jnp.dot(attended, weight[64 * head : 64 * head + 64, :], preferred_element_type=F32)
        total = term if total is None else total + term
    out[...] = total.astype(BF16).reshape(BLK, OWN, D)


def own_video(where, text):
    ids = where[1] * TOK + where[2] * OWN + lax.broadcasted_iota(jnp.int32, (OWN, 1), 0)
    return ids >= text[0]


def sum_blocks(got):
    total = got[0].astype(F32)
    for block in range(1, got.shape[0]):
        total = total + got[block].astype(F32)
    return total


def after_attention_kernel(where, text, got, tokens, mods, after, out):
    pick = picker(mods, own_video(where, text))
    residual = tokens[0, pl.ds(pl.multiple_of(where[2] * OWN, OWN), OWN), :].astype(F32)
    summed = residual + pick(2) * sum_blocks(got)
    after[...] = summed
    normed = (layer_norm(summed, 1e-05) * (1.0 + pick(4)) + pick(3)).astype(BF16)
    for block in range(GROUP):
        out[block] = normed


def feed_forward_kernel(rows, own, other, out, up, down, arrived):
    copies = []
    for part, weights in enumerate((own, other)):
        for side, near in enumerate((up, down)):
            far = weights.at[:, PIECE * side : PIECE * side + PIECE, :]
            copies.append(pltpu.make_async_copy(far, near.at[part], arrived.at[part, side]))
    for copy in copies:
        copy.start()
    block = rows[...].reshape(GROUP * OWN, D)
    result = None
    for part in range(2):
        copies[2 * part].wait()
        hidden = jnp.dot(block, up[part].reshape(D, UNITS), preferred_element_type=F32)
        activated = jax.nn.gelu(hidden, approximate=True).astype(BF16)
        copies[2 * part + 1].wait()
        term = lax.dot_general(activated, down[part].reshape(D, UNITS), ROWS_BY_ROWS, preferred_element_type=F32)
        result = term if result is None else result + term
    out[...] = result.astype(BF16).reshape(GROUP, OWN, D)


def pieces_kernel(up, down, out, arrived):
    copies = []
    for device in range(4):
        half = pl.ds(UNITS * (device % 2), UNITS)
        for side, weight in enumerate((up, down)):
            rows = pl.ds(PIECE * side, PIECE)
            copies.append(pltpu.make_async_copy(weight.at[:, half], out.at[device, rows, :], arrived.at[device, side]))
    for copy in copies:
        copy.start()
    for copy in copies:
        copy.wait()


def predict_kernel(where, text, got, after, mods, weight, hidden_out, predicted):
    pick = picker(mods, own_video(where, text))
    after_mlp = after[...] + pick(5) * sum_blocks(got)
    hidden_out[0] = after_mlp.astype(BF16)
    normed = (layer_norm(after_mlp, 1e-05) * (1.0 + pick(7)) + pick(6)).astype(BF16)
    predicted[...] = jnp.dot(normed, weight[...], preferred_element_type=F32)


def step_kernel(where, step, guidance, mine, other, latent, out):
    row = lax.broadcasted_iota(jnp.int32, (8, 128), 0)
    steps = row * 128 + lax.broadcasted_iota(jnp.int32, (8, 128), 1)
    low, high = math.sqrt(0.00085), math.sqrt(0.012)
    root_beta = low + steps.astype(F32) / 999.0 * (high - low)
    logs = jnp.log1p(-jnp.where(steps < 1000, root_beta * root_beta, 0.0))

    def alpha_bar(last):
        kept = jnp.where(steps <= last, logs, 0.0)
        return jnp.exp(jnp.sum(jnp.sum(kept, 1, keepdims=True), 0, keepdims=True))

    alpha_now = alpha_bar(step[0])
    alpha_prev = alpha_bar(step[0] - STRIDE)
    is_cond = where[0] == 0
    own, partner = mine[...], other[...]
    cond = jnp.where(is_cond, own, partner)
    uncond = jnp.where(is_cond, partner, own)
    both = uncond + guidance[0] * (cond - uncond)
    guided = jnp.where(is_cond, both[:, 0:32], both[:, 32:64])
    held = latent[...]
    root_now, root_rest = jnp.sqrt(alpha_now), jnp.sqrt(1.0 - alpha_now)
    clean = root_now * held - root_rest * guided
    noise = root_rest * held + root_now * guided
    out[...] = jnp.sqrt(alpha_prev) * clean + jnp.sqrt(1.0 - alpha_prev) * noise


ALONE = 60


def call(kernel, specs, shapes, mib=24, flops=10_000_000, scratch=()):
    return pl.pallas_call(
        kernel,
        out_shape=shapes,
        in_specs=specs,
        out_specs=jax.tree.map(lambda _: VMEM, shapes),
        scratch_shapes=scratch,
        compiler_params=pltpu.CompilerParams(vmem_limit_bytes=mib * 2**20),
        cost_estimate=pl.CostEstimate(flops=flops, bytes_accessed=4_000_000, transcendentals=0),
    )


def body(
    tokens_in,
    modulation,
    qk_gain,
    qkv_weight,
    out_weight,
    up_weight,
    down_weight,
    proj_weight,
    latent,
    text_count,
    positions,
    step_index,
    guidance,
):
    where = jnp.stack([lax.axis_index("cfg"), lax.axis_index(SEQ_AXES), lax.axis_index(BLK_AXES)]).astype(jnp.int32)

    pieces = call(
        pieces_kernel,
        [HBM, HBM],
        jax.ShapeDtypeStruct((4, 2 * PIECE, UNITS), BF16),
        mib=ALONE,
        scratch=[pltpu.SemaphoreType.DMA((4, 2))],
    )(up_weight, down_weight.T)
    pieces = lax.all_to_all(pieces, LINE, 0, 0, tiled=True)

    sent = call(
        project_kernel,
        [SMEM, SMEM] + [HBM] * 6,
        jax.ShapeDtypeStruct((SEQ, 80, 128), BF16),
        mib=ALONE,
        scratch=[
            pltpu.VMEM((1, TOK, D), BF16),
            pltpu.VMEM((2, 8, D), F32),
            pltpu.VMEM((2, 64), F32),
            pltpu.VMEM((3, TOK), jnp.int32),
            pltpu.VMEM((8, 128), F32),
            pltpu.VMEM((3, 192, D), BF16),
            pltpu.SemaphoreType.DMA((6,)),
        ],
    )(where, text_count, tokens_in, modulation, qk_gain, positions, jnp.asarray(frequencies()), qkv_weight)
    sent, pieces = lax.optimization_barrier((sent, pieces))
    weights = lax.all_gather(pieces, "z", axis=0, tiled=True)
    got = lax.all_to_all(sent, SEQ_AXES, 0, 0, tiled=True)
    attended = call(attend_kernel, [VMEM], jax.ShapeDtypeStruct((SEQ, 32, 128), BF16))(got)
    back = lax.all_to_all(attended, SEQ_AXES, 0, 0, tiled=True)
    blocks = jax.ShapeDtypeStruct((BLK, OWN, D), BF16)
    shared = jax.ShapeDtypeStruct((GROUP, OWN, D), BF16)
    partial = call(out_project_kernel, [VMEM, VMEM], blocks)(back, out_weight)
    partial = lax.all_to_all(partial, BLK_AXES, 0, 0, tiled=True)
    after, rows = call(
        after_attention_kernel,
        [SMEM, SMEM, VMEM, VMEM, VMEM],
        (jax.ShapeDtypeStruct((OWN, D), F32), shared),
    )(where, text_count, partial, tokens_in, modulation)
    rows, weights = lax.optimization_barrier((rows, weights))
    rows = lax.all_to_all(rows, SHARERS, 0, 0, tiled=True)
    swapped = lax.ppermute(weights, "core", [(0, 1), (1, 0)])
    both = pltpu.VMEM((2, SEQ, PIECE, UNITS), BF16)
    mlp = call(
        feed_forward_kernel,
        [VMEM, HBM, HBM],
        shared,
        mib=ALONE,
        scratch=[both, both, pltpu.SemaphoreType.DMA((2, 2))],
    )(rows, weights, swapped)
    mlp = lax.all_to_all(mlp, SHARERS, 0, 0, tiled=True)
    hidden_out, predicted = call(
        predict_kernel,
        [SMEM, SMEM, VMEM, VMEM, VMEM, VMEM],
        (jax.ShapeDtypeStruct((1, OWN, D), BF16), jax.ShapeDtypeStruct((OWN, 64), F32)),
    )(where, text_count, mlp, after, modulation, proj_weight)
    partner = lax.ppermute(predicted, "cfg", [(0, 1), (1, 0)])
    latent_prev = call(
        step_kernel,
        [SMEM, SMEM, SMEM, VMEM, VMEM, VMEM],
        jax.ShapeDtypeStruct((OWN, 32), F32),
    )(where, step_index, guidance, predicted, partner, latent)
    return (hidden_out, latent_prev)


def solution(mesh):
    devices = mesh.devices.reshape(2, 8, 2, 2, 4, 2)
    fine = jax.sharding.Mesh(devices, ("cfg", *SEQ_AXES, *BLK_AXES))
    rows = (*SEQ_AXES, *BLK_AXES)
    in_specs = (
        P("cfg", SEQ_AXES, None),
        P(),
        P(),
        P(None, BLK_AXES, None),
        P(BLK_AXES, None),
        P(SEQ_AXES, BLK_AXES),
        P(BLK_AXES, SEQ_AXES),
        P(),
        P(rows, "cfg"),
        P(),
        P(None, SEQ_AXES),
        P(),
        P(),
    )
    out_specs = (P("cfg", rows, None), P(rows, "cfg"))
    return jax.shard_map(body, mesh=fine, in_specs=in_specs, out_specs=out_specs, check_vma=False)
```

```python
import math

import jax
import jax.numpy as jnp
import numpy as np
from jax import lax
from jax.experimental import pallas as pl
from jax.experimental.pallas import tpu as pltpu
from jax.sharding import PartitionSpec as P

BF16 = jnp.bfloat16
F32 = jnp.float32
STRIDE = 20
TOK = 128
OWN = 16
D = 1536
UNITS = 384
SEQ = 32
BLK = 8
GROUP = 8
PIECE = 48

SEQ_AXES = ("z", "pair", "side")
LINE = ("pair", "side")
BLK_AXES = ("x", "core")
SHARERS = ("side", "x")

VMEM = pl.BlockSpec(memory_space=pltpu.VMEM)
SMEM = pl.BlockSpec(memory_space=pltpu.SMEM)
ANY = pl.BlockSpec(memory_space=pl.ANY)
HBM = pl.BlockSpec(memory_space=pltpu.HBM)

ROWS_BY_ROWS = (((1,), (1,)), ((), ()))


def frequencies():
    table = np.zeros((8, 128), np.float32)
    offset = 0
    for band, width in enumerate((16, 24, 24)):
        half = width // 2
        inverse = np.exp(-np.arange(half, dtype=np.float32) * np.float32(2.0 / width) * np.float32(math.log(10000.0)))
        for head in (0, 64):
            start = head + offset
            table[0, start : start + half] = inverse
            table[0, start + half : start + width] = inverse
            table[1, start : start + width] = band
            table[2, start : start + half] = 1.0
        offset += width
    return table


def layer_norm(values, epsilon):
    centered = values - jnp.mean(values, -1, keepdims=True)
    spread = jnp.mean(centered * centered, -1, keepdims=True)
    return centered * lax.rsqrt(spread + epsilon)


def picker(mods, video):
    return lambda row: jnp.where(video, mods[1, row : row + 1, :], mods[0, row : row + 1, :])


def project_kernel(place, text, step, tokens_far, mods_far, gain_far, positions_far, table_far, qkv_far, out, alphas, *scratch):
    tokens, mods, gain, positions, table, qkv, arrived = scratch
    far = (tokens_far, mods_far, gain_far, positions_far, table_far, qkv_far)
    copies = [pltpu.make_async_copy(a, b, arrived.at[i]) for i, (a, b) in enumerate(zip(far, scratch))]
    for copy in copies:
        copy.start()
    row = lax.broadcasted_iota(jnp.int32, (8, 128), 0)
    alphas[...] = jnp.where(row == 0, alpha_bar(step[0]), alpha_bar(step[0] - STRIDE))
    for copy in copies[:5]:
        copy.wait()
    ids = place[0] * TOK + lax.broadcasted_iota(jnp.int32, (TOK, 1), 0)
    video = ids >= text[0]
    pick = picker(mods, video)
    residual = tokens[0].astype(F32)
    normed = (layer_norm(residual, 1e-05) * (1.0 + pick(1)) + pick(0)).astype(BF16)

    def project(weight):
        return lax.dot_general(normed, weight, ROWS_BY_ROWS, preferred_element_type=F32)

    copies[5].wait()
    heads = project(qkv[0:2].reshape(384, D))
    values_low = project(qkv[2, 0:128, :])
    values_high = project(qkv[2, 64:192, :])

    lane = lax.broadcasted_iota(jnp.int32, (TOK, 128), 1)
    low = lane < 64
    band = table[1:2, :]
    where_at = positions[...].astype(F32)
    spread = [jnp.broadcast_to(where_at[a : a + 1, :], (128, 128)).T for a in range(3)]
    chosen = jnp.where(band == 0.0, spread[0], jnp.where(band == 1.0, spread[1], spread[2]))
    angles = chosen * table[0:1, :] * video.astype(F32)
    cosine = jnp.cos(angles)
    sine = jnp.sin(angles)
    first = table[2:3, :] > 0.5
    sine = jnp.where(first, -sine, sine)
    narrow = band == 0.0

    row_head = lax.broadcasted_iota(jnp.int32, (128, 128), 0) >> 6
    average = jnp.where(row_head == (lane >> 6), 1.0 / 64.0, 0.0)

    def head_mean(block):
        return jnp.dot(block, average, precision=lax.Precision.HIGHEST, preferred_element_type=F32)

    def prepare(block, gains):
        centered = block - head_mean(block)
        normal = centered * lax.rsqrt(head_mean(centered * centered) + 1e-06) * gains
        ahead = jnp.where(narrow, pltpu.roll(normal, 120, 1), pltpu.roll(normal, 116, 1))
        behind = jnp.where(narrow, pltpu.roll(normal, 8, 1), pltpu.roll(normal, 12, 1))
        return normal * cosine + jnp.where(first, ahead, behind) * sine

    query_gain = jnp.concatenate([gain[0:1, :], gain[0:1, :]], 1)
    key_gain = jnp.concatenate([gain[1:2, :], gain[1:2, :]], 1)
    mixed_gain = jnp.concatenate([gain[0:1, :], gain[1:2, :]], 1)
    queries_low = prepare(heads[:, 0:128], query_gain)
    query_and_key = prepare(heads[:, 128:256], mixed_gain)
    keys_high = prepare(heads[:, 256:384], key_gain)

    def turned(block):
        return pltpu.roll(block, 64, 1)

    pairs = [
        jnp.where(low, turned(query_and_key), turned(values_low)),
        jnp.where(low, keys_high, values_low),
        jnp.where(low, turned(keys_high), values_high),
    ]
    queries = [
        (queries_low, turned(queries_low)),
        (turned(queries_low), queries_low),
        (query_and_key, turned(query_and_key)),
    ]
    low16 = low[0:16, :]
    for head in range(3):
        pair = pairs[head].astype(BF16)
        left, right = queries[head]
        for part in range(4):
            start = 32 * part
            packed = jnp.where(low16, left[start : start + 16, :], right[start + 16 : start + 32, :])
            packed = (packed * 0.125).astype(BF16)
            for half in range(2):
                goes = 8 * head + 4 * half + part
                out[goes, 0:64, :] = pair[64 * half : 64 * half + 64, :]
                out[goes, 64:80, :] = packed
    out[24:32] = jnp.zeros((8, 80, 128), BF16)


def attend_kernel(got, out):
    pairs = got[:, 0:64, :].reshape(2048, 128)
    queries = got[:, 64:80, :].reshape(512, 128).astype(F32)
    lane = lax.broadcasted_iota(jnp.int32, (256, 128), 1)
    low = lane < 64
    for side in range(2):
        turned = queries if side == 0 else pltpu.roll(queries, 64, 1)
        for chunk in range(2):
            block = jnp.where(low, turned[256 * chunk : 256 * chunk + 256, :], 0.0).astype(BF16)
            scores = lax.dot_general(block, pairs, ROWS_BY_ROWS, preferred_element_type=F32)
            highest = jnp.max(scores, -1, keepdims=True)
            weights = jnp.exp(scores - highest)
            total = jnp.sum(weights, -1, keepdims=True)
            mixed = jnp.dot(weights.astype(BF16), pairs, preferred_element_type=F32) / total
            level = highest + jnp.log(total)
            coarse = level.astype(BF16).astype(F32)
            medium = (level - coarse).astype(BF16).astype(F32)
            fine = level - coarse - medium
            parts = jnp.where(lane == 0, coarse, jnp.where(lane == 1, medium, fine))
            result = jnp.where(low, parts, mixed).astype(BF16)
            out[16 * chunk : 16 * chunk + 16, 16 * side : 16 * side + 16, :] = result.reshape(16, 16, 128)


def out_project_kernel(got, weight, out):
    total = None
    for head in range(3):
        sides = []
        for half in range(2):
            first = 8 * head + 4 * half
            block = got[first : first + 4].reshape(TOK, 128).astype(F32)
            level = block[:, 0:1] + block[:, 1:2] + block[:, 2:3]
            sides.append((block, level))
        (one, level_one), (two, level_two) = sides
        highest = jnp.maximum(level_one, level_two)
        share_one = jnp.exp(level_one - highest)
        share_two = jnp.exp(level_two - highest)
        mixed = (one * share_one + two * share_two) / (share_one + share_two)
        attended = mixed[:, 64:128].astype(BF16)
        term = jnp.dot(attended, weight[64 * head : 64 * head + 64, :], preferred_element_type=F32)
        total = term if total is None else total + term
    out[...] = total.astype(BF16).reshape(BLK, OWN, D)


def own_video(place, part, text):
    ids = place[0] * TOK + part[0] * OWN + lax.broadcasted_iota(jnp.int32, (OWN, 1), 0)
    return ids >= text[0]


def sum_blocks(got):
    total = got[0].astype(F32)
    for block in range(1, got.shape[0]):
        total = total + got[block].astype(F32)
    return total


def after_attention_kernel(place, part, text, got, tokens, mods, after, out):
    pick = picker(mods, own_video(place, part, text))
    residual = tokens[0, pl.ds(pl.multiple_of(part[0] * OWN, OWN), OWN), :].astype(F32)
    summed = residual + pick(2) * sum_blocks(got)
    after[...] = summed
    normed = (layer_norm(summed, 1e-05) * (1.0 + pick(4)) + pick(3)).astype(BF16)
    for block in range(GROUP):
        out[block] = normed


def feed_forward_kernel(rows, weights, out, up, down, arrived):
    def fetch(part, side):
        far = weights.at[pl.ds(SEQ * part, SEQ), PIECE * side : PIECE * side + PIECE, :]
        return pltpu.make_async_copy(far, (up, down)[side].at[part], arrived.at[part, side])

    fetch(0, 0).start()
    fetch(0, 1).start()
    block = rows[...].reshape(GROUP * OWN, D)
    result = None
    for part in range(2):
        fetch(part, 0).wait()
        if part == 0:
            fetch(1, 0).start()
        hidden = jnp.dot(block, up[part].reshape(D, UNITS), preferred_element_type=F32)
        activated = jax.nn.gelu(hidden, approximate=True).astype(BF16)
        fetch(part, 1).wait()
        if part == 0:
            fetch(1, 1).start()
        term = lax.dot_general(activated, down[part].reshape(D, UNITS), ROWS_BY_ROWS, preferred_element_type=F32)
        result = term if result is None else result + term
    out[...] = result.astype(BF16).reshape(GROUP, OWN, D)


def pieces_kernel(up, down, out, arrived):
    copies = []
    for device in range(4):
        half = pl.ds(UNITS * (device % 2), UNITS)
        for side, weight in enumerate((up, down)):
            rows = pl.ds(PIECE * side, PIECE)
            copies.append(pltpu.make_async_copy(weight.at[:, half], out.at[device, rows, :], arrived.at[device, side]))
    for copy in copies:
        copy.start()
    for copy in copies:
        copy.wait()


def predict_kernel(place, part, text, got, after, mods, weight, hidden_out, predicted):
    pick = picker(mods, own_video(place, part, text))
    after_mlp = after[...] + pick(5) * sum_blocks(got)
    hidden_out[0] = after_mlp.astype(BF16)
    normed = (layer_norm(after_mlp, 1e-05) * (1.0 + pick(7)) + pick(6)).astype(BF16)
    predicted[...] = jnp.dot(normed, weight[...], preferred_element_type=F32)


def alpha_bar(last):
    row = lax.broadcasted_iota(jnp.int32, (8, 128), 0)
    steps = row * 128 + lax.broadcasted_iota(jnp.int32, (8, 128), 1)
    low, high = math.sqrt(0.00085), math.sqrt(0.012)
    root_beta = low + steps.astype(F32) / 999.0 * (high - low)
    kept = jnp.where(steps <= last, jnp.log1p(-jnp.where(steps < 1000, root_beta * root_beta, 0.0)), 0.0)
    return jnp.exp(jnp.sum(jnp.sum(kept, 1, keepdims=True), 0, keepdims=True))


def step_kernel(branch, guidance, alphas, mine, other, latent, out):
    alpha_now, alpha_prev = alphas[0:1, 0:1], alphas[1:2, 0:1]
    is_cond = branch[0] == 0
    own, partner = mine[...], other[...]
    cond = jnp.where(is_cond, own, partner)
    uncond = jnp.where(is_cond, partner, own)
    both = uncond + guidance[0] * (cond - uncond)
    guided = jnp.where(is_cond, both[:, 0:32], both[:, 32:64])
    held = latent[...]
    root_now, root_rest = jnp.sqrt(alpha_now), jnp.sqrt(1.0 - alpha_now)
    clean = root_now * held - root_rest * guided
    noise = root_rest * held + root_now * guided
    out[...] = jnp.sqrt(alpha_prev) * clean + jnp.sqrt(1.0 - alpha_prev) * noise


ALONE = 60


def call(kernel, specs, shapes, mib=24, result=VMEM, scratch=()):
    return pl.pallas_call(
        kernel,
        out_shape=shapes,
        in_specs=specs,
        out_specs=jax.tree.map(lambda _: result, shapes),
        scratch_shapes=scratch,
        compiler_params=pltpu.CompilerParams(vmem_limit_bytes=mib * 2**20),
        cost_estimate=pl.CostEstimate(flops=10_000_000, bytes_accessed=4_000_000, transcendentals=0),
    )


def body(
    tokens_in,
    modulation,
    qk_gain,
    qkv_weight,
    out_weight,
    up_weight,
    down_weight,
    proj_weight,
    latent,
    text_count,
    positions,
    step_index,
    guidance,
):
    branch, place, part = (lax.axis_index(axes).reshape(1) for axes in ("cfg", SEQ_AXES, BLK_AXES))

    pieces = call(
        pieces_kernel,
        [HBM, HBM],
        jax.ShapeDtypeStruct((4, 2 * PIECE, UNITS), BF16),
        mib=ALONE,
        result=HBM,
        scratch=[pltpu.SemaphoreType.DMA((4, 2))],
    )(up_weight, down_weight.T)
    pieces = lax.all_to_all(pieces, LINE, 0, 0, tiled=True)

    sent, alphas = call(
        project_kernel,
        [SMEM, SMEM, SMEM] + [HBM] * 6,
        (jax.ShapeDtypeStruct((SEQ, 80, 128), BF16), jax.ShapeDtypeStruct((8, 128), F32)),
        mib=ALONE,
        scratch=[
            pltpu.VMEM((1, TOK, D), BF16),
            pltpu.VMEM((2, 8, D), F32),
            pltpu.VMEM((2, 64), F32),
            pltpu.VMEM((3, TOK), jnp.int32),
            pltpu.VMEM((8, 128), F32),
            pltpu.VMEM((3, 192, D), BF16),
            pltpu.SemaphoreType.DMA((6,)),
        ],
    )(place, text_count, step_index, tokens_in, modulation, qk_gain, positions, jnp.asarray(frequencies()), qkv_weight)
    sent, pieces = lax.optimization_barrier((sent, pieces))
    weights = lax.all_gather(pieces, "z", axis=0, tiled=True)
    weights = lax.all_gather(weights, "core", axis=0, tiled=True)
    got = lax.all_to_all(sent, SEQ_AXES, 0, 0, tiled=True)
    attended = call(attend_kernel, [VMEM], jax.ShapeDtypeStruct((SEQ, 32, 128), BF16))(got)
    back = lax.all_to_all(attended, SEQ_AXES, 0, 0, tiled=True)
    blocks = jax.ShapeDtypeStruct((BLK, OWN, D), BF16)
    shared = jax.ShapeDtypeStruct((GROUP, OWN, D), BF16)
    partial = call(out_project_kernel, [VMEM, VMEM], blocks)(back, out_weight)
    partial = lax.all_to_all(partial, BLK_AXES, 0, 0, tiled=True)
    after, rows = call(
        after_attention_kernel,
        [SMEM, SMEM, SMEM, VMEM, VMEM, VMEM],
        (jax.ShapeDtypeStruct((OWN, D), F32), shared),
    )(place, part, text_count, partial, tokens_in, modulation)
    rows = lax.all_to_all(rows, SHARERS, 0, 0, tiled=True)
    both = pltpu.VMEM((2, SEQ, PIECE, UNITS), BF16)
    mlp = call(
        feed_forward_kernel,
        [VMEM, HBM],
        shared,
        mib=ALONE,
        scratch=[both, both, pltpu.SemaphoreType.DMA((2, 2))],
    )(rows, weights)
    mlp = lax.all_to_all(mlp, SHARERS, 0, 0, tiled=True)
    hidden_out, predicted = call(
        predict_kernel,
        [SMEM, SMEM, SMEM, VMEM, VMEM, VMEM, VMEM],
        (jax.ShapeDtypeStruct((1, OWN, D), BF16), jax.ShapeDtypeStruct((OWN, 64), F32)),
    )(place, part, text_count, mlp, after, modulation, proj_weight)
    partner = lax.ppermute(predicted, "cfg", [(0, 1), (1, 0)])
    latent_prev = call(
        step_kernel,
        [SMEM, SMEM, VMEM, VMEM, VMEM, VMEM],
        jax.ShapeDtypeStruct((OWN, 32), F32),
    )(branch, guidance, alphas, predicted, partner, latent)
    return (hidden_out, latent_prev)


def solution(mesh):
    devices = mesh.devices.reshape(2, 8, 2, 2, 4, 2)
    fine = jax.sharding.Mesh(devices, ("cfg", *SEQ_AXES, *BLK_AXES))
    rows = (*SEQ_AXES, *BLK_AXES)
    in_specs = (
        P("cfg", SEQ_AXES, None),
        P(),
        P(),
        P(None, BLK_AXES, None),
        P(BLK_AXES, None),
        P(SEQ_AXES, BLK_AXES),
        P(BLK_AXES, SEQ_AXES),
        P(),
        P(rows, "cfg"),
        P(),
        P(None, SEQ_AXES),
        P(),
        P(),
    )
    out_specs = (P("cfg", rows, None), P(rows, "cfg"))
    return jax.shard_map(body, mesh=fine, in_specs=in_specs, out_specs=out_specs, check_vma=False)
```

```python
import math

import jax
import jax.numpy as jnp
import numpy as np
from jax import lax
from jax.experimental import pallas as pl
from jax.experimental.pallas import tpu as pltpu
from jax.sharding import PartitionSpec as P

BF16 = jnp.bfloat16
F32 = jnp.float32
STRIDE = 20
TOK = 128
OWN = 16
D = 1536
UNITS = 384
SEQ = 32
BLK = 8
GROUP = 8
PIECE = 48

SEQ_AXES = ("z", "pair", "side")
LINE = ("pair", "side")
BLK_AXES = ("x", "core")
SHARERS = ("side", "x")

VMEM = pl.BlockSpec(memory_space=pltpu.VMEM)
SMEM = pl.BlockSpec(memory_space=pltpu.SMEM)
ANY = pl.BlockSpec(memory_space=pl.ANY)
HBM = pl.BlockSpec(memory_space=pltpu.HBM)

ROWS_BY_ROWS = (((1,), (1,)), ((), ()))


def frequencies():
    table = np.zeros((8, 128), np.float32)
    offset = 0
    for band, width in enumerate((16, 24, 24)):
        half = width // 2
        inverse = np.exp(-np.arange(half, dtype=np.float32) * np.float32(2.0 / width) * np.float32(math.log(10000.0)))
        for head in (0, 64):
            start = head + offset
            table[0, start : start + half] = inverse
            table[0, start + half : start + width] = inverse
            table[1, start : start + width] = band
            table[2, start : start + half] = 1.0
        offset += width
    return table


def layer_norm(values, epsilon):
    centered = values - jnp.mean(values, -1, keepdims=True)
    spread = jnp.mean(centered * centered, -1, keepdims=True)
    return centered * lax.rsqrt(spread + epsilon)


def picker(mods, video):
    return lambda row: jnp.where(video, mods[1, row : row + 1, :], mods[0, row : row + 1, :])


def project_kernel(place, text, step, tokens_far, mods_far, gain_far, positions_far, table_far, qkv_far, out, alphas, *scratch):
    tokens, mods, gain, positions, table, qkv, arrived = scratch
    far = (tokens_far, mods_far, gain_far, positions_far, table_far, qkv_far)
    copies = [pltpu.make_async_copy(a, b, arrived.at[i]) for i, (a, b) in enumerate(zip(far, scratch))]
    for copy in copies:
        copy.start()
    row = lax.broadcasted_iota(jnp.int32, (8, 128), 0)
    alphas[...] = jnp.where(row == 0, alpha_bar(step[0]), alpha_bar(step[0] - STRIDE))
    for copy in copies[:5]:
        copy.wait()
    ids = place[0] * TOK + lax.broadcasted_iota(jnp.int32, (TOK, 1), 0)
    video = ids >= text[0]
    pick = picker(mods, video)
    residual = tokens[0].astype(F32)
    normed = (layer_norm(residual, 1e-05) * (1.0 + pick(1)) + pick(0)).astype(BF16)

    def project(weight):
        return lax.dot_general(normed, weight, ROWS_BY_ROWS, preferred_element_type=F32)

    copies[5].wait()
    heads = project(qkv[0:2].reshape(384, D))
    values_low = project(qkv[2, 0:128, :])
    values_high = project(qkv[2, 64:192, :])

    lane = lax.broadcasted_iota(jnp.int32, (TOK, 128), 1)
    low = lane < 64
    band = table[1:2, :]
    where_at = positions[...].astype(F32)
    spread = [jnp.broadcast_to(where_at[a : a + 1, :], (128, 128)).T for a in range(3)]
    chosen = jnp.where(band == 0.0, spread[0], jnp.where(band == 1.0, spread[1], spread[2]))
    angles = chosen * table[0:1, :] * video.astype(F32)
    cosine = jnp.cos(angles)
    sine = jnp.sin(angles)
    first = table[2:3, :] > 0.5
    sine = jnp.where(first, -sine, sine)
    narrow = band == 0.0

    row_head = lax.broadcasted_iota(jnp.int32, (128, 128), 0) >> 6
    average = jnp.where(row_head == (lane >> 6), 1.0 / 64.0, 0.0)

    def head_mean(block):
        return jnp.dot(block, average, precision=lax.Precision.HIGHEST, preferred_element_type=F32)

    def prepare(block, gains):
        centered = block - head_mean(block)
        normal = centered * lax.rsqrt(head_mean(centered * centered) + 1e-06) * gains
        ahead = jnp.where(narrow, pltpu.roll(normal, 120, 1), pltpu.roll(normal, 116, 1))
        behind = jnp.where(narrow, pltpu.roll(normal, 8, 1), pltpu.roll(normal, 12, 1))
        return normal * cosine + jnp.where(first, ahead, behind) * sine

    query_gain = jnp.concatenate([gain[0:1, :], gain[0:1, :]], 1)
    key_gain = jnp.concatenate([gain[1:2, :], gain[1:2, :]], 1)
    mixed_gain = jnp.concatenate([gain[0:1, :], gain[1:2, :]], 1)
    queries_low = prepare(heads[:, 0:128], query_gain)
    query_and_key = prepare(heads[:, 128:256], mixed_gain)
    keys_high = prepare(heads[:, 256:384], key_gain)

    def turned(block):
        return pltpu.roll(block, 64, 1)

    pairs = [
        jnp.where(low, turned(query_and_key), turned(values_low)),
        jnp.where(low, keys_high, values_low),
        jnp.where(low, turned(keys_high), values_high),
    ]
    queries = [
        (queries_low, turned(queries_low)),
        (turned(queries_low), queries_low),
        (query_and_key, turned(query_and_key)),
    ]
    low16 = low[0:16, :]
    for head in range(3):
        pair = pairs[head].astype(BF16)
        left, right = queries[head]
        for part in range(4):
            start = 32 * part
            packed = jnp.where(low16, left[start : start + 16, :], right[start + 16 : start + 32, :])
            packed = (packed * 0.125).astype(BF16)
            for half in range(2):
                goes = 8 * head + 4 * half + part
                out[goes, 0:64, :] = pair[64 * half : 64 * half + 64, :]
                out[goes, 64:80, :] = packed
    out[24:32] = jnp.zeros((8, 80, 128), BF16)


def attend_kernel(got, out):
    pairs = got[:, 0:64, :].reshape(2048, 128)
    queries = got[:, 64:80, :].reshape(512, 128).astype(F32)
    lane = lax.broadcasted_iota(jnp.int32, (256, 128), 1)
    low = lane < 64
    for side in range(2):
        turned = queries if side == 0 else pltpu.roll(queries, 64, 1)
        for chunk in range(2):
            block = jnp.where(low, turned[256 * chunk : 256 * chunk + 256, :], 0.0).astype(BF16)
            scores = lax.dot_general(block, pairs, ROWS_BY_ROWS, preferred_element_type=F32)
            highest = jnp.max(scores, -1, keepdims=True)
            weights = jnp.exp(scores - highest)
            total = jnp.sum(weights, -1, keepdims=True)
            mixed = jnp.dot(weights.astype(BF16), pairs, preferred_element_type=F32) / total
            level = highest + jnp.log(total)
            coarse = level.astype(BF16).astype(F32)
            medium = (level - coarse).astype(BF16).astype(F32)
            fine = level - coarse - medium
            parts = jnp.where(lane == 0, coarse, jnp.where(lane == 1, medium, fine))
            result = jnp.where(low, parts, mixed).astype(BF16)
            out[16 * chunk : 16 * chunk + 16, 16 * side : 16 * side + 16, :] = result.reshape(16, 16, 128)


def out_project_kernel(got, weight, out):
    total = None
    for head in range(3):
        sides = []
        for half in range(2):
            first = 8 * head + 4 * half
            block = got[first : first + 4].reshape(TOK, 128).astype(F32)
            level = block[:, 0:1] + block[:, 1:2] + block[:, 2:3]
            sides.append((block, level))
        (one, level_one), (two, level_two) = sides
        highest = jnp.maximum(level_one, level_two)
        share_one = jnp.exp(level_one - highest)
        share_two = jnp.exp(level_two - highest)
        mixed = (one * share_one + two * share_two) / (share_one + share_two)
        attended = mixed[:, 64:128].astype(BF16)
        term = jnp.dot(attended, weight[64 * head : 64 * head + 64, :], preferred_element_type=F32)
        total = term if total is None else total + term
    out[...] = total.astype(BF16).reshape(BLK, OWN, D)


def own_video(place, part, text):
    ids = place[0] * TOK + part[0] * OWN + lax.broadcasted_iota(jnp.int32, (OWN, 1), 0)
    return ids >= text[0]


def sum_blocks(got):
    total = got[0].astype(F32)
    for block in range(1, got.shape[0]):
        total = total + got[block].astype(F32)
    return total


def after_attention_kernel(place, part, text, got, tokens, mods, after, out):
    pick = picker(mods, own_video(place, part, text))
    residual = tokens[0, pl.ds(pl.multiple_of(part[0] * OWN, OWN), OWN), :].astype(F32)
    summed = residual + pick(2) * sum_blocks(got)
    after[...] = summed
    normed = (layer_norm(summed, 1e-05) * (1.0 + pick(4)) + pick(3)).astype(BF16)
    for block in range(GROUP):
        out[block] = normed


def feed_forward_kernel(rows, own, other, out):
    block = rows[...].reshape(GROUP * OWN, D)
    result = None
    for weights in (other, own):
        up = weights[:, 0:PIECE, :].reshape(D, UNITS)
        down = weights[:, PIECE : 2 * PIECE, :].reshape(D, UNITS)
        hidden = jnp.dot(block, up, preferred_element_type=F32)
        activated = jax.nn.gelu(hidden, approximate=True).astype(BF16)
        term = lax.dot_general(activated, down, ROWS_BY_ROWS, preferred_element_type=F32)
        result = term if result is None else result + term
    out[...] = result.astype(BF16).reshape(GROUP, OWN, D)


def pieces_kernel(up, down, out, arrived):
    copies = []
    for device in range(4):
        half = pl.ds(UNITS * (device % 2), UNITS)
        for side, weight in enumerate((up, down)):
            rows = pl.ds(PIECE * side, PIECE)
            copies.append(pltpu.make_async_copy(weight.at[:, half], out.at[device, rows, :], arrived.at[device, side]))
    for copy in copies:
        copy.start()
    for copy in copies:
        copy.wait()


def predict_kernel(place, part, text, got, after, mods, weight, hidden_out, predicted):
    pick = picker(mods, own_video(place, part, text))
    after_mlp = after[...] + pick(5) * sum_blocks(got)
    hidden_out[0] = after_mlp.astype(BF16)
    normed = (layer_norm(after_mlp, 1e-05) * (1.0 + pick(7)) + pick(6)).astype(BF16)
    predicted[...] = lax.dot_general(normed, weight[...], ROWS_BY_ROWS, preferred_element_type=F32)


def alpha_bar(last):
    row = lax.broadcasted_iota(jnp.int32, (8, 128), 0)
    steps = row * 128 + lax.broadcasted_iota(jnp.int32, (8, 128), 1)
    low, high = math.sqrt(0.00085), math.sqrt(0.012)
    root_beta = low + steps.astype(F32) / 999.0 * (high - low)
    kept = jnp.where(steps <= last, jnp.log1p(-jnp.where(steps < 1000, root_beta * root_beta, 0.0)), 0.0)
    return jnp.exp(jnp.sum(jnp.sum(kept, 1, keepdims=True), 0, keepdims=True))


def step_kernel(branch, guidance, alphas, mine, other, latent, out):
    alpha_now, alpha_prev = alphas[0:1, 0:1], alphas[1:2, 0:1]
    is_cond = branch[0] == 0
    own, partner = mine[...], other[...]
    cond = jnp.where(is_cond, own, partner)
    uncond = jnp.where(is_cond, partner, own)
    both = uncond + guidance[0] * (cond - uncond)
    guided = jnp.where(is_cond, both[:, 0:32], both[:, 32:64])
    held = latent[...]
    root_now, root_rest = jnp.sqrt(alpha_now), jnp.sqrt(1.0 - alpha_now)
    clean = root_now * held - root_rest * guided
    noise = root_rest * held + root_now * guided
    out[...] = jnp.sqrt(alpha_prev) * clean + jnp.sqrt(1.0 - alpha_prev) * noise


ALONE = 60


def call(kernel, specs, shapes, mib=24, scratch=()):
    return pl.pallas_call(
        kernel,
        out_shape=shapes,
        in_specs=specs,
        out_specs=jax.tree.map(lambda _: VMEM, shapes),
        scratch_shapes=scratch,
        compiler_params=pltpu.CompilerParams(vmem_limit_bytes=mib * 2**20),
        cost_estimate=pl.CostEstimate(flops=10_000_000, bytes_accessed=4_000_000, transcendentals=0),
    )


def body(
    tokens_in,
    modulation,
    qk_gain,
    qkv_weight,
    out_weight,
    up_weight,
    down_weight,
    proj_weight,
    latent,
    text_count,
    positions,
    step_index,
    guidance,
):
    branch, place, part = (lax.axis_index(axes).reshape(1) for axes in ("cfg", SEQ_AXES, BLK_AXES))

    pieces = call(
        pieces_kernel,
        [HBM, HBM],
        jax.ShapeDtypeStruct((4, 2 * PIECE, UNITS), BF16),
        mib=ALONE,
        scratch=[pltpu.SemaphoreType.DMA((4, 2))],
    )(up_weight, down_weight.T)
    pieces = lax.all_to_all(pieces, LINE, 0, 0, tiled=True)

    sent, alphas = call(
        project_kernel,
        [SMEM, SMEM, SMEM] + [HBM] * 6,
        (jax.ShapeDtypeStruct((SEQ, 80, 128), BF16), jax.ShapeDtypeStruct((8, 128), F32)),
        mib=ALONE,
        scratch=[
            pltpu.VMEM((1, TOK, D), BF16),
            pltpu.VMEM((2, 8, D), F32),
            pltpu.VMEM((2, 64), F32),
            pltpu.VMEM((3, TOK), jnp.int32),
            pltpu.VMEM((8, 128), F32),
            pltpu.VMEM((3, 192, D), BF16),
            pltpu.SemaphoreType.DMA((6,)),
        ],
    )(place, text_count, step_index, tokens_in, modulation, qk_gain, positions, jnp.asarray(frequencies()), qkv_weight)
    sent, pieces, branch, part = lax.optimization_barrier((sent, pieces, branch, part))
    weights = lax.all_gather(pieces, "z", axis=0, tiled=True)
    got = lax.all_to_all(sent, SEQ_AXES, 0, 0, tiled=True)
    attended = call(attend_kernel, [VMEM], jax.ShapeDtypeStruct((SEQ, 32, 128), BF16))(got)
    back = lax.all_to_all(attended, SEQ_AXES, 0, 0, tiled=True)
    blocks = jax.ShapeDtypeStruct((BLK, OWN, D), BF16)
    shared = jax.ShapeDtypeStruct((GROUP, OWN, D), BF16)
    partial = call(out_project_kernel, [VMEM, VMEM], blocks)(back, out_weight)
    partial = lax.all_to_all(partial, BLK_AXES, 0, 0, tiled=True)
    after, rows = call(
        after_attention_kernel,
        [SMEM, SMEM, SMEM, VMEM, VMEM, VMEM],
        (jax.ShapeDtypeStruct((OWN, D), F32), shared),
    )(place, part, text_count, partial, tokens_in, modulation)
    rows, weights = lax.optimization_barrier((rows, weights))
    rows = lax.all_to_all(rows, SHARERS, 0, 0, tiled=True)
    swapped = lax.ppermute(weights, "core", [(0, 1), (1, 0)])
    mlp = call(feed_forward_kernel, [VMEM, VMEM, VMEM], shared)(rows, weights, swapped)
    mlp = lax.all_to_all(mlp, SHARERS, 0, 0, tiled=True)
    hidden_out, predicted = call(
        predict_kernel,
        [SMEM, SMEM, SMEM, VMEM, VMEM, VMEM, VMEM],
        (jax.ShapeDtypeStruct((1, OWN, D), BF16), jax.ShapeDtypeStruct((OWN, 64), F32)),
    )(place, part, text_count, mlp, after, modulation, proj_weight.T)
    partner = lax.ppermute(predicted, "cfg", [(0, 1), (1, 0)])
    latent_prev = call(
        step_kernel,
        [SMEM, SMEM, VMEM, VMEM, VMEM, VMEM],
        jax.ShapeDtypeStruct((OWN, 32), F32),
    )(branch, guidance, alphas, predicted, partner, latent)
    return (hidden_out, latent_prev)


def solution(mesh):
    devices = mesh.devices.reshape(2, 8, 2, 2, 4, 2)
    fine = jax.sharding.Mesh(devices, ("cfg", *SEQ_AXES, *BLK_AXES))
    rows = (*SEQ_AXES, *BLK_AXES)
    in_specs = (
        P("cfg", SEQ_AXES, None),
        P(),
        P(),
        P(None, BLK_AXES, None),
        P(BLK_AXES, None),
        P(SEQ_AXES, BLK_AXES),
        P(BLK_AXES, SEQ_AXES),
        P(),
        P(rows, "cfg"),
        P(),
        P(None, SEQ_AXES),
        P(),
        P(),
    )
    out_specs = (P("cfg", rows, None), P(rows, "cfg"))
    return jax.shard_map(body, mesh=fine, in_specs=in_specs, out_specs=out_specs, check_vma=False)
```

```python
import math

import jax
import jax.numpy as jnp
import numpy as np
from jax import lax
from jax.experimental import pallas as pl
from jax.experimental.pallas import tpu as pltpu
from jax.sharding import PartitionSpec as P

BF16 = jnp.bfloat16
F32 = jnp.float32
STRIDE = 20
TOK = 128
OWN = 16
D = 1536
UNITS = 384
SEQ = 32
BLK = 8
GROUP = 8
PIECE = 48

SEQ_AXES = ("z", "pair", "side")
LINE = ("pair", "side")
BLK_AXES = ("x", "core")
SHARERS = ("side", "x")

VMEM = pl.BlockSpec(memory_space=pltpu.VMEM)
SMEM = pl.BlockSpec(memory_space=pltpu.SMEM)
ANY = pl.BlockSpec(memory_space=pl.ANY)
HBM = pl.BlockSpec(memory_space=pltpu.HBM)

ROWS_BY_ROWS = (((1,), (1,)), ((), ()))


def frequencies():
    table = np.zeros((8, 128), np.float32)
    offset = 0
    for band, width in enumerate((16, 24, 24)):
        half = width // 2
        inverse = np.exp(-np.arange(half, dtype=np.float32) * np.float32(2.0 / width) * np.float32(math.log(10000.0)))
        for head in (0, 64):
            start = head + offset
            table[0, start : start + half] = inverse
            table[0, start + half : start + width] = inverse
            table[1, start : start + width] = band
            table[2, start : start + half] = 1.0
        offset += width
    return table


def layer_norm(values, epsilon):
    centered = values - jnp.mean(values, -1, keepdims=True)
    spread = jnp.mean(centered * centered, -1, keepdims=True)
    return centered * lax.rsqrt(spread + epsilon)


def picker(mods, video):
    return lambda row: jnp.where(video, mods[1, row : row + 1, :], mods[0, row : row + 1, :])


def project_kernel(place, text, step, tokens_far, mods_far, gain_far, positions_far, table_far, qkv_far, out, alphas, *scratch):
    tokens, mods, gain, positions, table, qkv, arrived = scratch
    far = (tokens_far, mods_far, gain_far, positions_far, table_far, qkv_far)
    copies = [pltpu.make_async_copy(a, b, arrived.at[i]) for i, (a, b) in enumerate(zip(far, scratch))]
    for copy in copies:
        copy.start()
    row = lax.broadcasted_iota(jnp.int32, (8, 128), 0)
    alphas[...] = jnp.where(row == 0, alpha_bar(step[0]), alpha_bar(step[0] - STRIDE))
    for copy in copies[:5]:
        copy.wait()
    ids = place[0] * TOK + lax.broadcasted_iota(jnp.int32, (TOK, 1), 0)
    video = ids >= text[0]
    pick = picker(mods, video)
    residual = tokens[0].astype(F32)
    normed = (layer_norm(residual, 1e-05) * (1.0 + pick(1)) + pick(0)).astype(BF16)

    def project(weight):
        return lax.dot_general(normed, weight, ROWS_BY_ROWS, preferred_element_type=F32)

    copies[5].wait()
    heads = project(qkv[0:2].reshape(384, D))
    values_low = project(qkv[2, 0:128, :])
    values_high = project(qkv[2, 64:192, :])

    lane = lax.broadcasted_iota(jnp.int32, (TOK, 128), 1)
    low = lane < 64
    band = table[1:2, :]
    where_at = positions[...].astype(F32)
    spread = [jnp.broadcast_to(where_at[a : a + 1, :], (128, 128)).T for a in range(3)]
    chosen = jnp.where(band == 0.0, spread[0], jnp.where(band == 1.0, spread[1], spread[2]))
    angles = chosen * table[0:1, :] * video.astype(F32)
    cosine = jnp.cos(angles)
    sine = jnp.sin(angles)
    first = table[2:3, :] > 0.5
    sine = jnp.where(first, -sine, sine)
    narrow = band == 0.0

    row_head = lax.broadcasted_iota(jnp.int32, (128, 128), 0) >> 6
    average = jnp.where(row_head == (lane >> 6), 1.0 / 64.0, 0.0)

    def head_mean(block):
        return jnp.dot(block, average, precision=lax.Precision.HIGHEST, preferred_element_type=F32)

    def prepare(block, gains):
        centered = block - head_mean(block)
        normal = centered * lax.rsqrt(head_mean(centered * centered) + 1e-06) * gains
        ahead = jnp.where(narrow, pltpu.roll(normal, 120, 1), pltpu.roll(normal, 116, 1))
        behind = jnp.where(narrow, pltpu.roll(normal, 8, 1), pltpu.roll(normal, 12, 1))
        return normal * cosine + jnp.where(first, ahead, behind) * sine

    query_gain = jnp.concatenate([gain[0:1, :], gain[0:1, :]], 1)
    key_gain = jnp.concatenate([gain[1:2, :], gain[1:2, :]], 1)
    mixed_gain = jnp.concatenate([gain[0:1, :], gain[1:2, :]], 1)
    queries_low = prepare(heads[:, 0:128], query_gain)
    query_and_key = prepare(heads[:, 128:256], mixed_gain)
    keys_high = prepare(heads[:, 256:384], key_gain)

    def turned(block):
        return pltpu.roll(block, 64, 1)

    pairs = [
        jnp.where(low, turned(query_and_key), turned(values_low)),
        jnp.where(low, keys_high, values_low),
        jnp.where(low, turned(keys_high), values_high),
    ]
    queries = [
        (queries_low, turned(queries_low)),
        (turned(queries_low), queries_low),
        (query_and_key, turned(query_and_key)),
    ]
    low16 = low[0:16, :]
    for head in range(3):
        pair = pairs[head].astype(BF16)
        left, right = queries[head]
        for part in range(4):
            start = 32 * part
            packed = jnp.where(low16, left[start : start + 16, :], right[start + 16 : start + 32, :])
            packed = (packed * 0.125).astype(BF16)
            for half in range(2):
                goes = 8 * head + 4 * half + part
                out[goes, 0:64, :] = pair[64 * half : 64 * half + 64, :]
                out[goes, 64:80, :] = packed
    out[24:32] = jnp.zeros((8, 80, 128), BF16)


def attend_kernel(got, out):
    pairs = got[:, 0:64, :].reshape(2048, 128)
    queries = got[:, 64:80, :].reshape(512, 128).astype(F32)
    lane = lax.broadcasted_iota(jnp.int32, (256, 128), 1)
    low = lane < 64
    for side in range(2):
        turned = queries if side == 0 else pltpu.roll(queries, 64, 1)
        for chunk in range(2):
            block = jnp.where(low, turned[256 * chunk : 256 * chunk + 256, :], 0.0).astype(BF16)
            scores = lax.dot_general(block, pairs, ROWS_BY_ROWS, preferred_element_type=F32)
            highest = jnp.max(scores, -1, keepdims=True)
            weights = jnp.exp(scores - highest)
            total = jnp.sum(weights, -1, keepdims=True)
            mixed = jnp.dot(weights.astype(BF16), pairs, preferred_element_type=F32) / total
            level = highest + jnp.log(total)
            coarse = level.astype(BF16).astype(F32)
            medium = (level - coarse).astype(BF16).astype(F32)
            fine = level - coarse - medium
            parts = jnp.where(lane == 0, coarse, jnp.where(lane == 1, medium, fine))
            result = jnp.where(low, parts, mixed).astype(BF16)
            out[16 * chunk : 16 * chunk + 16, 16 * side : 16 * side + 16, :] = result.reshape(16, 16, 128)


def out_project_kernel(got, weight, out):
    total = None
    for head in range(3):
        sides = []
        for half in range(2):
            first = 8 * head + 4 * half
            block = got[first : first + 4].reshape(TOK, 128).astype(F32)
            level = block[:, 0:1] + block[:, 1:2] + block[:, 2:3]
            sides.append((block, level))
        (one, level_one), (two, level_two) = sides
        highest = jnp.maximum(level_one, level_two)
        share_one = jnp.exp(level_one - highest)
        share_two = jnp.exp(level_two - highest)
        mixed = (one * share_one + two * share_two) / (share_one + share_two)
        attended = mixed[:, 64:128].astype(BF16)
        term = jnp.dot(attended, weight[64 * head : 64 * head + 64, :], preferred_element_type=F32)
        total = term if total is None else total + term
    out[...] = total.astype(BF16).reshape(BLK, OWN, D)


def own_video(place, part, text):
    ids = place[0] * TOK + part[0] * OWN + lax.broadcasted_iota(jnp.int32, (OWN, 1), 0)
    return ids >= text[0]


def sum_blocks(got):
    total = got[0].astype(F32)
    for block in range(1, got.shape[0]):
        total = total + got[block].astype(F32)
    return total


def after_attention_kernel(place, part, text, got, tokens, mods, after, out):
    pick = picker(mods, own_video(place, part, text))
    residual = tokens[0, pl.ds(pl.multiple_of(part[0] * OWN, OWN), OWN), :].astype(F32)
    summed = residual + pick(2) * sum_blocks(got)
    after[...] = summed
    normed = (layer_norm(summed, 1e-05) * (1.0 + pick(4)) + pick(3)).astype(BF16)
    for block in range(GROUP):
        out[block] = normed


def feed_forward_kernel(rows, own, other, out):
    block = rows[...].reshape(GROUP * OWN, D)
    result = None
    for weights in (other, own):
        up = weights[:, 0:PIECE, :].reshape(D, UNITS)
        down = weights[:, PIECE : 2 * PIECE, :].reshape(D, UNITS)
        hidden = jnp.dot(block, up, preferred_element_type=F32)
        activated = jax.nn.gelu(hidden, approximate=True).astype(BF16)
        term = lax.dot_general(activated, down, ROWS_BY_ROWS, preferred_element_type=F32)
        result = term if result is None else result + term
    out[...] = result.astype(BF16).reshape(GROUP, OWN, D)


def assemble_kernel(place, *refs):
    blocks, out = refs[:9], refs[9]
    for block, away, start in zip(blocks, (0, -1, -2, -3, -4, 1, 2, 3, 4), (0, 0, 0, 0, 0, 0, 0, 0, 2)):
        first = (place[0] // 4 + 8 + away) % 8 * 4 + start
        out[pl.ds(first, block.shape[0])] = block[...]


def pieces_kernel(up, down, out, arrived):
    copies = []
    for device in range(4):
        half = pl.ds(UNITS * (device % 2), UNITS)
        for side, weight in enumerate((up, down)):
            rows = pl.ds(PIECE * side, PIECE)
            copies.append(pltpu.make_async_copy(weight.at[:, half], out.at[device, rows, :], arrived.at[device, side]))
    for copy in copies:
        copy.start()
    for copy in copies:
        copy.wait()


def predict_kernel(place, part, text, got, after, mods, weight, hidden_out, predicted):
    pick = picker(mods, own_video(place, part, text))
    after_mlp = after[...] + pick(5) * sum_blocks(got)
    hidden_out[0] = after_mlp.astype(BF16)
    normed = (layer_norm(after_mlp, 1e-05) * (1.0 + pick(7)) + pick(6)).astype(BF16)
    predicted[...] = lax.dot_general(normed, weight[...], ROWS_BY_ROWS, preferred_element_type=F32)


def alpha_bar(last):
    row = lax.broadcasted_iota(jnp.int32, (8, 128), 0)
    steps = row * 128 + lax.broadcasted_iota(jnp.int32, (8, 128), 1)
    low, high = math.sqrt(0.00085), math.sqrt(0.012)
    root_beta = low + steps.astype(F32) / 999.0 * (high - low)
    kept = jnp.where(steps <= last, jnp.log1p(-jnp.where(steps < 1000, root_beta * root_beta, 0.0)), 0.0)
    return jnp.exp(jnp.sum(jnp.sum(kept, 1, keepdims=True), 0, keepdims=True))


def step_kernel(branch, guidance, alphas, mine, other, latent, out):
    alpha_now, alpha_prev = alphas[0:1, 0:1], alphas[1:2, 0:1]
    is_cond = branch[0] == 0
    own, partner = mine[...], other[...]
    cond = jnp.where(is_cond, own, partner)
    uncond = jnp.where(is_cond, partner, own)
    both = uncond + guidance[0] * (cond - uncond)
    guided = jnp.where(is_cond, both[:, 0:32], both[:, 32:64])
    held = latent[...]
    root_now, root_rest = jnp.sqrt(alpha_now), jnp.sqrt(1.0 - alpha_now)
    clean = root_now * held - root_rest * guided
    noise = root_rest * held + root_now * guided
    out[...] = jnp.sqrt(alpha_prev) * clean + jnp.sqrt(1.0 - alpha_prev) * noise


ALONE = 60


def call(kernel, specs, shapes, mib=24, scratch=()):
    return pl.pallas_call(
        kernel,
        out_shape=shapes,
        in_specs=specs,
        out_specs=jax.tree.map(lambda _: VMEM, shapes),
        scratch_shapes=scratch,
        compiler_params=pltpu.CompilerParams(vmem_limit_bytes=mib * 2**20),
        cost_estimate=pl.CostEstimate(flops=10_000_000, bytes_accessed=4_000_000, transcendentals=0),
    )


def body(
    tokens_in,
    modulation,
    qk_gain,
    qkv_weight,
    out_weight,
    up_weight,
    down_weight,
    proj_weight,
    latent,
    text_count,
    positions,
    step_index,
    guidance,
):
    branch, place, part = (lax.axis_index(axes).reshape(1) for axes in ("cfg", SEQ_AXES, BLK_AXES))

    pieces = call(
        pieces_kernel,
        [HBM, HBM],
        jax.ShapeDtypeStruct((4, 2 * PIECE, UNITS), BF16),
        mib=ALONE,
        scratch=[pltpu.SemaphoreType.DMA((4, 2))],
    )(up_weight, down_weight.T)
    pieces = lax.all_to_all(pieces, LINE, 0, 0, tiled=True)

    def shifted(block, step):
        return lax.ppermute(block, "z", [(z, (z + step) % 8) for z in range(8)])

    sent, alphas = call(
        project_kernel,
        [SMEM, SMEM, SMEM] + [HBM] * 6,
        (jax.ShapeDtypeStruct((SEQ, 80, 128), BF16), jax.ShapeDtypeStruct((8, 128), F32)),
        mib=ALONE,
        scratch=[
            pltpu.VMEM((1, TOK, D), BF16),
            pltpu.VMEM((2, 8, D), F32),
            pltpu.VMEM((2, 64), F32),
            pltpu.VMEM((3, TOK), jnp.int32),
            pltpu.VMEM((8, 128), F32),
            pltpu.VMEM((3, 192, D), BF16),
            pltpu.SemaphoreType.DMA((6,)),
        ],
    )(place, text_count, step_index, tokens_in, modulation, qk_gain, positions, jnp.asarray(frequencies()), qkv_weight)
    sent, pieces, branch, part = lax.optimization_barrier((sent, pieces, branch, part))
    got = lax.all_to_all(sent, SEQ_AXES, 0, 0, tiled=True)
    below, above = [shifted(pieces, 1)], [shifted(pieces, -1)]
    got, below, above = lax.optimization_barrier((got, below, above))
    attended = call(attend_kernel, [VMEM], jax.ShapeDtypeStruct((SEQ, 32, 128), BF16))(got)
    attended, below, above = lax.optimization_barrier((attended, below, above))
    back = lax.all_to_all(attended, SEQ_AXES, 0, 0, tiled=True)
    below.append(shifted(below[0], 1))
    above.append(shifted(above[0], -1))
    back, below, above = lax.optimization_barrier((back, below, above))
    blocks = jax.ShapeDtypeStruct((BLK, OWN, D), BF16)
    shared = jax.ShapeDtypeStruct((GROUP, OWN, D), BF16)
    partial = call(out_project_kernel, [VMEM, VMEM], blocks)(back, out_weight)
    partial, below, above = lax.optimization_barrier((partial, below, above))
    partial = lax.all_to_all(partial, BLK_AXES, 0, 0, tiled=True)
    below.append(shifted(below[1], 1))
    above.append(shifted(above[1], -1))
    below.append(shifted(below[2][0:2], 1))
    above.append(shifted(above[2][2:4], -1))
    partial, below, above = lax.optimization_barrier((partial, below, above))
    after, rows = call(
        after_attention_kernel,
        [SMEM, SMEM, SMEM, VMEM, VMEM, VMEM],
        (jax.ShapeDtypeStruct((OWN, D), F32), shared),
    )(place, part, text_count, partial, tokens_in, modulation)
    weights = call(
        assemble_kernel,
        [SMEM] + [VMEM] * 9,
        jax.ShapeDtypeStruct((SEQ, 2 * PIECE, UNITS), BF16),
    )(place, pieces, *below, *above)
    rows, weights = lax.optimization_barrier((rows, weights))
    rows = lax.all_to_all(rows, SHARERS, 0, 0, tiled=True)
    swapped = lax.ppermute(weights, "core", [(0, 1), (1, 0)])
    mlp = call(feed_forward_kernel, [VMEM, VMEM, VMEM], shared)(rows, weights, swapped)
    mlp = lax.all_to_all(mlp, SHARERS, 0, 0, tiled=True)
    hidden_out, predicted = call(
        predict_kernel,
        [SMEM, SMEM, SMEM, VMEM, VMEM, VMEM, VMEM],
        (jax.ShapeDtypeStruct((1, OWN, D), BF16), jax.ShapeDtypeStruct((OWN, 64), F32)),
    )(place, part, text_count, mlp, after, modulation, proj_weight.T)
    partner = lax.ppermute(predicted, "cfg", [(0, 1), (1, 0)])
    latent_prev = call(
        step_kernel,
        [SMEM, SMEM, VMEM, VMEM, VMEM, VMEM],
        jax.ShapeDtypeStruct((OWN, 32), F32),
    )(branch, guidance, alphas, predicted, partner, latent)
    return (hidden_out, latent_prev)


def solution(mesh):
    devices = mesh.devices.reshape(2, 8, 2, 2, 4, 2)
    fine = jax.sharding.Mesh(devices, ("cfg", *SEQ_AXES, *BLK_AXES))
    rows = (*SEQ_AXES, *BLK_AXES)
    in_specs = (
        P("cfg", SEQ_AXES, None),
        P(),
        P(),
        P(None, BLK_AXES, None),
        P(BLK_AXES, None),
        P(SEQ_AXES, BLK_AXES),
        P(BLK_AXES, SEQ_AXES),
        P(),
        P(rows, "cfg"),
        P(),
        P(None, SEQ_AXES),
        P(),
        P(),
    )
    out_specs = (P("cfg", rows, None), P(rows, "cfg"))
    return jax.shard_map(body, mesh=fine, in_specs=in_specs, out_specs=out_specs, check_vma=False)
```

```python
import math

import jax
import jax.numpy as jnp
import numpy as np
from jax import lax
from jax.experimental import pallas as pl
from jax.experimental.pallas import tpu as pltpu
from jax.sharding import PartitionSpec as P

BF16 = jnp.bfloat16
F32 = jnp.float32
STRIDE = 20
TOK = 128
OWN = 16
D = 1536
UNITS = 384
SEQ = 32
BLK = 8
GROUP = 8
PIECE = 48

SEQ_AXES = ("z", "pair", "side")
LINE = ("pair", "side")
BLK_AXES = ("x", "core")
SHARERS = ("side", "x")

VMEM = pl.BlockSpec(memory_space=pltpu.VMEM)
SMEM = pl.BlockSpec(memory_space=pltpu.SMEM)
ANY = pl.BlockSpec(memory_space=pl.ANY)
HBM = pl.BlockSpec(memory_space=pltpu.HBM)

ROWS_BY_ROWS = (((1,), (1,)), ((), ()))


def frequencies():
    table = np.zeros((8, 128), np.float32)
    offset = 0
    for band, width in enumerate((16, 24, 24)):
        half = width // 2
        inverse = np.exp(-np.arange(half, dtype=np.float32) * np.float32(2.0 / width) * np.float32(math.log(10000.0)))
        for head in (0, 64):
            start = head + offset
            table[0, start : start + half] = inverse
            table[0, start + half : start + width] = inverse
            table[1, start : start + width] = band
            table[2, start : start + half] = 1.0
        offset += width
    return table


def index_of(axes):
    index = 0
    for axis in axes:
        index = index * lax.axis_size(axis) + lax.axis_index(axis)
    return index


def layer_norm(values, epsilon):
    centered = values - jnp.mean(values, -1, keepdims=True)
    spread = jnp.mean(centered * centered, -1, keepdims=True)
    return centered * lax.rsqrt(spread + epsilon)


def picker(mods, video):
    return lambda row: jnp.where(video, mods[1, row : row + 1, :], mods[0, row : row + 1, :])


def project_kernel(text, step, tokens_far, mods_far, gain_far, positions_far, table_far, qkv_far, out, alphas, *scratch):
    tokens, mods, gain, positions, table, qkv, arrived = scratch
    far = (tokens_far, mods_far, gain_far, positions_far, table_far, qkv_far)
    copies = [pltpu.make_async_copy(a, b, arrived.at[i]) for i, (a, b) in enumerate(zip(far, scratch))]
    for copy in copies:
        copy.start()
    row = lax.broadcasted_iota(jnp.int32, (8, 128), 0)
    alphas[...] = jnp.where(row == 0, alpha_bar(step[0]), alpha_bar(step[0] - STRIDE))
    for copy in copies[:5]:
        copy.wait()
    ids = index_of(SEQ_AXES) * TOK + lax.broadcasted_iota(jnp.int32, (TOK, 1), 0)
    video = ids >= text[0]
    pick = picker(mods, video)
    residual = tokens[0].astype(F32)
    normed = (layer_norm(residual, 1e-05) * (1.0 + pick(1)) + pick(0)).astype(BF16)

    def project(weight):
        return lax.dot_general(normed, weight, ROWS_BY_ROWS, preferred_element_type=F32)

    copies[5].wait()
    heads = project(qkv[0:2].reshape(384, D))
    values_low = project(qkv[2, 0:128, :])
    values_high = project(qkv[2, 64:192, :])

    lane = lax.broadcasted_iota(jnp.int32, (TOK, 128), 1)
    low = lane < 64
    band = table[1:2, :]
    where_at = positions[...].astype(F32)
    spread = [jnp.broadcast_to(where_at[a : a + 1, :], (128, 128)).T for a in range(3)]
    chosen = jnp.where(band == 0.0, spread[0], jnp.where(band == 1.0, spread[1], spread[2]))
    angles = chosen * table[0:1, :] * video.astype(F32)
    cosine = jnp.cos(angles)
    sine = jnp.sin(angles)
    first = table[2:3, :] > 0.5
    sine = jnp.where(first, -sine, sine)
    narrow = band == 0.0

    row_head = lax.broadcasted_iota(jnp.int32, (128, 128), 0) >> 6
    average = jnp.where(row_head == (lane >> 6), 1.0 / 64.0, 0.0)

    def head_mean(block):
        return jnp.dot(block, average, precision=lax.Precision.HIGHEST, preferred_element_type=F32)

    def prepare(block, gains):
        centered = block - head_mean(block)
        normal = centered * lax.rsqrt(head_mean(centered * centered) + 1e-06) * gains
        ahead = jnp.where(narrow, pltpu.roll(normal, 120, 1), pltpu.roll(normal, 116, 1))
        behind = jnp.where(narrow, pltpu.roll(normal, 8, 1), pltpu.roll(normal, 12, 1))
        return normal * cosine + jnp.where(first, ahead, behind) * sine

    query_gain = jnp.concatenate([gain[0:1, :], gain[0:1, :]], 1)
    key_gain = jnp.concatenate([gain[1:2, :], gain[1:2, :]], 1)
    mixed_gain = jnp.concatenate([gain[0:1, :], gain[1:2, :]], 1)
    queries_low = prepare(heads[:, 0:128], query_gain)
    query_and_key = prepare(heads[:, 128:256], mixed_gain)
    keys_high = prepare(heads[:, 256:384], key_gain)

    def turned(block):
        return pltpu.roll(block, 64, 1)

    pairs = [
        jnp.where(low, turned(query_and_key), turned(values_low)),
        jnp.where(low, keys_high, values_low),
        jnp.where(low, turned(keys_high), values_high),
    ]
    queries = [
        (queries_low, turned(queries_low)),
        (turned(queries_low), queries_low),
        (query_and_key, turned(query_and_key)),
    ]
    low16 = low[0:16, :]
    for head in range(3):
        pair = pairs[head].astype(BF16)
        left, right = queries[head]
        for part in range(4):
            start = 32 * part
            packed = jnp.where(low16, left[start : start + 16, :], right[start + 16 : start + 32, :])
            packed = (packed * 0.125).astype(BF16)
            for half in range(2):
                goes = 8 * head + 4 * half + part
                out[goes, 0:64, :] = pair[64 * half : 64 * half + 64, :]
                out[goes, 64:80, :] = packed
    out[24:32] = jnp.zeros((8, 80, 128), BF16)


def attend_kernel(got, out):
    pairs = got[:, 0:64, :].reshape(2048, 128)
    queries = got[:, 64:80, :].reshape(512, 128).astype(F32)
    lane = lax.broadcasted_iota(jnp.int32, (256, 128), 1)
    low = lane < 64
    for side in range(2):
        turned = queries if side == 0 else pltpu.roll(queries, 64, 1)
        for chunk in range(2):
            block = jnp.where(low, turned[256 * chunk : 256 * chunk + 256, :], 0.0).astype(BF16)
            scores = lax.dot_general(block, pairs, ROWS_BY_ROWS, preferred_element_type=F32)
            highest = jnp.max(scores, -1, keepdims=True)
            weights = jnp.exp(scores - highest)
            total = jnp.sum(weights, -1, keepdims=True)
            mixed = jnp.dot(weights.astype(BF16), pairs, preferred_element_type=F32) / total
            level = highest + jnp.log(total)
            coarse = level.astype(BF16).astype(F32)
            medium = (level - coarse).astype(BF16).astype(F32)
            fine = level - coarse - medium
            parts = jnp.where(lane == 0, coarse, jnp.where(lane == 1, medium, fine))
            result = jnp.where(low, parts, mixed).astype(BF16)
            out[16 * chunk : 16 * chunk + 16, 16 * side : 16 * side + 16, :] = result.reshape(16, 16, 128)


def out_project_kernel(got, weight, out):
    total = None
    for head in range(3):
        sides = []
        for half in range(2):
            first = 8 * head + 4 * half
            block = got[first : first + 4].reshape(TOK, 128).astype(F32)
            level = block[:, 0:1] + block[:, 1:2] + block[:, 2:3]
            sides.append((block, level))
        (one, level_one), (two, level_two) = sides
        highest = jnp.maximum(level_one, level_two)
        share_one = jnp.exp(level_one - highest)
        share_two = jnp.exp(level_two - highest)
        mixed = (one * share_one + two * share_two) / (share_one + share_two)
        attended = mixed[:, 64:128].astype(BF16)
        term = jnp.dot(attended, weight[64 * head : 64 * head + 64, :], preferred_element_type=F32)
        total = term if total is None else total + term
    out[...] = total.astype(BF16).reshape(BLK, OWN, D)


def own_video(text):
    ids = index_of(SEQ_AXES) * TOK + index_of(BLK_AXES) * OWN + lax.broadcasted_iota(jnp.int32, (OWN, 1), 0)
    return ids >= text[0]


def sum_blocks(got):
    total = got[0].astype(F32)
    for block in range(1, got.shape[0]):
        total = total + got[block].astype(F32)
    return total


def after_attention_kernel(text, got, tokens, mods, after, out):
    pick = picker(mods, own_video(text))
    residual = tokens[0, pl.ds(pl.multiple_of(index_of(BLK_AXES) * OWN, OWN), OWN), :].astype(F32)
    summed = residual + pick(2) * sum_blocks(got)
    after[...] = summed
    normed = (layer_norm(summed, 1e-05) * (1.0 + pick(4)) + pick(3)).astype(BF16)
    for block in range(GROUP):
        out[block] = normed


def feed_forward_kernel(rows, own, other, out):
    block = rows[...].reshape(GROUP * OWN, D)
    result = None
    for weights in (other, own):
        up = weights[:, 0:PIECE, :].reshape(D, UNITS)
        down = weights[:, PIECE : 2 * PIECE, :].reshape(D, UNITS)
        hidden = jnp.dot(block, up, preferred_element_type=F32)
        activated = jax.nn.gelu(hidden, approximate=True).astype(BF16)
        term = lax.dot_general(activated, down, ROWS_BY_ROWS, preferred_element_type=F32)
        result = term if result is None else result + term
    out[...] = result.astype(BF16).reshape(GROUP, OWN, D)


def pieces_kernel(up, down, out, arrived):
    copies = []
    for device in range(4):
        half = pl.ds(UNITS * (device % 2), UNITS)
        for side, weight in enumerate((up, down)):
            rows = pl.ds(PIECE * side, PIECE)
            copies.append(pltpu.make_async_copy(weight.at[:, half], out.at[device, rows, :], arrived.at[device, side]))
    for copy in copies:
        copy.start()
    for copy in copies:
        copy.wait()


def predict_kernel(text, got, after, mods, weight, hidden_out, predicted):
    pick = picker(mods, own_video(text))
    after_mlp = after[...] + pick(5) * sum_blocks(got)
    hidden_out[0] = after_mlp.astype(BF16)
    normed = (layer_norm(after_mlp, 1e-05) * (1.0 + pick(7)) + pick(6)).astype(BF16)
    predicted[...] = lax.dot_general(normed, weight[...], ROWS_BY_ROWS, preferred_element_type=F32)


def alpha_bar(last):
    row = lax.broadcasted_iota(jnp.int32, (8, 128), 0)
    steps = row * 128 + lax.broadcasted_iota(jnp.int32, (8, 128), 1)
    low, high = math.sqrt(0.00085), math.sqrt(0.012)
    root_beta = low + steps.astype(F32) / 999.0 * (high - low)
    kept = jnp.where(steps <= last, jnp.log1p(-jnp.where(steps < 1000, root_beta * root_beta, 0.0)), 0.0)
    return jnp.exp(jnp.sum(jnp.sum(kept, 1, keepdims=True), 0, keepdims=True))


def step_kernel(guidance, alphas, mine, other, latent, out):
    alpha_now, alpha_prev = alphas[0:1, 0:1], alphas[1:2, 0:1]
    is_cond = lax.axis_index("cfg") == 0
    own, partner = mine[...], other[...]
    cond = jnp.where(is_cond, own, partner)
    uncond = jnp.where(is_cond, partner, own)
    both = uncond + guidance[0] * (cond - uncond)
    guided = jnp.where(is_cond, both[:, 0:32], both[:, 32:64])
    held = latent[...]
    root_now, root_rest = jnp.sqrt(alpha_now), jnp.sqrt(1.0 - alpha_now)
    clean = root_now * held - root_rest * guided
    noise = root_rest * held + root_now * guided
    out[...] = jnp.sqrt(alpha_prev) * clean + jnp.sqrt(1.0 - alpha_prev) * noise


ALONE = 63


def call(kernel, specs, shapes, mib=24, scratch=()):
    return pl.pallas_call(
        kernel,
        out_shape=shapes,
        in_specs=specs,
        out_specs=jax.tree.map(lambda _: VMEM, shapes),
        scratch_shapes=scratch,
        compiler_params=pltpu.CompilerParams(vmem_limit_bytes=mib * 2**20),
        cost_estimate=pl.CostEstimate(flops=10_000_000, bytes_accessed=4_000_000, transcendentals=0),
    )


def body(
    tokens_in,
    modulation,
    qk_gain,
    qkv_weight,
    out_weight,
    up_weight,
    down_weight,
    proj_weight,
    latent,
    text_count,
    positions,
    step_index,
    guidance,
):
    pieces = call(
        pieces_kernel,
        [HBM, HBM],
        jax.ShapeDtypeStruct((4, 2 * PIECE, UNITS), BF16),
        mib=ALONE,
        scratch=[pltpu.SemaphoreType.DMA((4, 2))],
    )(up_weight, down_weight.T)
    pieces = lax.all_to_all(pieces, LINE, 0, 0, tiled=True)

    sent, alphas = call(
        project_kernel,
        [SMEM, SMEM] + [HBM] * 6,
        (jax.ShapeDtypeStruct((SEQ, 80, 128), BF16), jax.ShapeDtypeStruct((8, 128), F32)),
        mib=ALONE,
        scratch=[
            pltpu.VMEM((1, TOK, D), BF16),
            pltpu.VMEM((2, 8, D), F32),
            pltpu.VMEM((2, 64), F32),
            pltpu.VMEM((3, TOK), jnp.int32),
            pltpu.VMEM((8, 128), F32),
            pltpu.VMEM((3, 192, D), BF16),
            pltpu.SemaphoreType.DMA((6,)),
        ],
    )(text_count, step_index, tokens_in, modulation, qk_gain, positions, jnp.asarray(frequencies()), qkv_weight)
    sent, pieces = lax.optimization_barrier((sent, pieces))
    weights = lax.all_gather(pieces, "z", axis=0, tiled=True)
    got = lax.all_to_all(sent, SEQ_AXES, 0, 0, tiled=True)
    attended = call(attend_kernel, [VMEM], jax.ShapeDtypeStruct((SEQ, 32, 128), BF16))(got)
    back = lax.all_to_all(attended, SEQ_AXES, 0, 0, tiled=True)
    blocks = jax.ShapeDtypeStruct((BLK, OWN, D), BF16)
    shared = jax.ShapeDtypeStruct((GROUP, OWN, D), BF16)
    partial = call(out_project_kernel, [VMEM, VMEM], blocks)(back, out_weight)
    partial = lax.all_to_all(partial, BLK_AXES, 0, 0, tiled=True)
    after, rows = call(
        after_attention_kernel,
        [SMEM, VMEM, VMEM, VMEM],
        (jax.ShapeDtypeStruct((OWN, D), F32), shared),
    )(text_count, partial, tokens_in, modulation)
    rows, weights = lax.optimization_barrier((rows, weights))
    rows = lax.all_to_all(rows, SHARERS, 0, 0, tiled=True)
    swapped = lax.ppermute(weights, "core", [(0, 1), (1, 0)])
    mlp = call(feed_forward_kernel, [VMEM, VMEM, VMEM], shared)(rows, weights, swapped)
    mlp = lax.all_to_all(mlp, SHARERS, 0, 0, tiled=True)
    hidden_out, predicted = call(
        predict_kernel,
        [SMEM, VMEM, VMEM, VMEM, VMEM],
        (jax.ShapeDtypeStruct((1, OWN, D), BF16), jax.ShapeDtypeStruct((OWN, 64), F32)),
    )(text_count, mlp, after, modulation, proj_weight.T)
    partner = lax.ppermute(predicted, "cfg", [(0, 1), (1, 0)])
    latent_prev = call(
        step_kernel,
        [SMEM, VMEM, VMEM, VMEM, VMEM],
        jax.ShapeDtypeStruct((OWN, 32), F32),
    )(guidance, alphas, predicted, partner, latent)
    return (hidden_out, latent_prev)


def solution(mesh):
    devices = mesh.devices.reshape(2, 8, 2, 2, 4, 2)
    fine = jax.sharding.Mesh(devices, ("cfg", *SEQ_AXES, *BLK_AXES))
    rows = (*SEQ_AXES, *BLK_AXES)
    in_specs = (
        P("cfg", SEQ_AXES, None),
        P(),
        P(),
        P(None, BLK_AXES, None),
        P(BLK_AXES, None),
        P(SEQ_AXES, BLK_AXES),
        P(BLK_AXES, SEQ_AXES),
        P(),
        P(rows, "cfg"),
        P(),
        P(None, SEQ_AXES),
        P(),
        P(),
    )
    out_specs = (P("cfg", rows, None), P(rows, "cfg"))
    return jax.shard_map(body, mesh=fine, in_specs=in_specs, out_specs=out_specs, check_vma=False)
```

```python
import math

import jax
import jax.numpy as jnp
import numpy as np
from jax import lax
from jax.experimental import pallas as pl
from jax.experimental.pallas import tpu as pltpu
from jax.sharding import PartitionSpec as P

BF16 = jnp.bfloat16
F32 = jnp.float32
STRIDE = 20
TOK = 128
OWN = 16
D = 1536
UNITS = 384
SEQ = 32
BLK = 8
GROUP = 8
PIECE = 48

SEQ_AXES = ("z", "pair", "side")
LINE = ("pair", "side")
BLK_AXES = ("x", "core")
SHARERS = ("side", "x")

VMEM = pl.BlockSpec(memory_space=pltpu.VMEM)
SMEM = pl.BlockSpec(memory_space=pltpu.SMEM)
ANY = pl.BlockSpec(memory_space=pl.ANY)
HBM = pl.BlockSpec(memory_space=pltpu.HBM)

ROWS_BY_ROWS = (((1,), (1,)), ((), ()))


def frequencies():
    table = np.zeros((8, 128), np.float32)
    offset = 0
    for band, width in enumerate((16, 24, 24)):
        half = width // 2
        inverse = np.exp(-np.arange(half, dtype=np.float32) * np.float32(2.0 / width) * np.float32(math.log(10000.0)))
        for head in (0, 64):
            start = head + offset
            table[0, start : start + half] = inverse
            table[0, start + half : start + width] = inverse
            table[1, start : start + width] = band
            table[2, start : start + half] = 1.0
        offset += width
    return table


def index_of(axes):
    index = 0
    for axis in axes:
        index = index * lax.axis_size(axis) + lax.axis_index(axis)
    return index


def layer_norm(values, epsilon):
    centered = values - jnp.mean(values, -1, keepdims=True)
    spread = jnp.mean(centered * centered, -1, keepdims=True)
    return centered * lax.rsqrt(spread + epsilon)


def picker(mods, video):
    return lambda row: jnp.where(video, mods[1, row : row + 1, :], mods[0, row : row + 1, :])


def project_kernel(text, step, tokens_far, mods_far, gain_far, positions_far, table_far, qkv_far, out, alphas, *scratch):
    tokens, mods, gain, positions, table, qkv, arrived = scratch
    far = (tokens_far, mods_far, gain_far, positions_far, table_far, qkv_far)
    copies = [pltpu.make_async_copy(a, b, arrived.at[i]) for i, (a, b) in enumerate(zip(far, scratch))]
    for copy in copies:
        copy.start()
    row = lax.broadcasted_iota(jnp.int32, (8, 128), 0)
    alphas[...] = jnp.where(row == 0, alpha_bar(step[0]), alpha_bar(step[0] - STRIDE))
    for copy in copies[:5]:
        copy.wait()
    ids = index_of(SEQ_AXES) * TOK + lax.broadcasted_iota(jnp.int32, (TOK, 1), 0)
    video = ids >= text[0]
    pick = picker(mods, video)
    residual = tokens[0].astype(F32)
    normed = (layer_norm(residual, 1e-05) * (1.0 + pick(1)) + pick(0)).astype(BF16)

    def project(weight):
        return lax.dot_general(normed, weight, ROWS_BY_ROWS, preferred_element_type=F32)

    copies[5].wait()
    heads = project(qkv[0:2].reshape(384, D))
    values_low = project(qkv[2, 0:128, :])
    values_high = project(qkv[2, 64:192, :])

    lane = lax.broadcasted_iota(jnp.int32, (TOK, 128), 1)
    low = lane < 64
    band = table[1:2, :]
    where_at = positions[...].astype(F32)
    spread = [jnp.broadcast_to(where_at[a : a + 1, :], (128, 128)).T for a in range(3)]
    chosen = jnp.where(band == 0.0, spread[0], jnp.where(band == 1.0, spread[1], spread[2]))
    angles = chosen * table[0:1, :] * video.astype(F32)
    cosine = jnp.cos(angles)
    sine = jnp.sin(angles)
    first = table[2:3, :] > 0.5
    sine = jnp.where(first, -sine, sine)
    narrow = band == 0.0

    row_head = lax.broadcasted_iota(jnp.int32, (128, 128), 0) >> 6
    average = jnp.where(row_head == (lane >> 6), 1.0 / 64.0, 0.0)

    def head_mean(block):
        return jnp.dot(block, average, precision=lax.Precision.HIGHEST, preferred_element_type=F32)

    def prepare(block, gains):
        centered = block - head_mean(block)
        normal = centered * lax.rsqrt(head_mean(centered * centered) + 1e-06) * gains
        ahead = jnp.where(narrow, pltpu.roll(normal, 120, 1), pltpu.roll(normal, 116, 1))
        behind = jnp.where(narrow, pltpu.roll(normal, 8, 1), pltpu.roll(normal, 12, 1))
        return normal * cosine + jnp.where(first, ahead, behind) * sine

    query_gain = jnp.concatenate([gain[0:1, :], gain[0:1, :]], 1)
    key_gain = jnp.concatenate([gain[1:2, :], gain[1:2, :]], 1)
    mixed_gain = jnp.concatenate([gain[0:1, :], gain[1:2, :]], 1)
    queries_low = prepare(heads[:, 0:128], query_gain)
    query_and_key = prepare(heads[:, 128:256], mixed_gain)
    keys_high = prepare(heads[:, 256:384], key_gain)

    def turned(block):
        return pltpu.roll(block, 64, 1)

    pairs = [
        jnp.where(low, turned(query_and_key), turned(values_low)),
        jnp.where(low, keys_high, values_low),
        jnp.where(low, turned(keys_high), values_high),
    ]
    queries = [
        (queries_low, turned(queries_low)),
        (turned(queries_low), queries_low),
        (query_and_key, turned(query_and_key)),
    ]
    low16 = low[0:16, :]
    for head in range(3):
        pair = pairs[head].astype(BF16)
        left, right = queries[head]
        for part in range(4):
            start = 32 * part
            packed = jnp.where(low16, left[start : start + 16, :], right[start + 16 : start + 32, :])
            packed = (packed * 0.125).astype(BF16)
            for half in range(2):
                goes = 8 * head + 4 * half + part
                out[goes, 0:64, :] = pair[64 * half : 64 * half + 64, :]
                out[goes, 64:80, :] = packed
    out[24:32] = jnp.zeros((8, 80, 128), BF16)


def attend_kernel(got, out):
    pairs = got[:, 0:64, :].reshape(2048, 128)
    queries = got[:, 64:80, :].reshape(512, 128).astype(F32)
    lane = lax.broadcasted_iota(jnp.int32, (256, 128), 1)
    low = lane < 64
    for side in range(2):
        turned = queries if side == 0 else pltpu.roll(queries, 64, 1)
        for chunk in range(2):
            block = jnp.where(low, turned[256 * chunk : 256 * chunk + 256, :], 0.0).astype(BF16)
            scores = lax.dot_general(block, pairs, ROWS_BY_ROWS, preferred_element_type=F32)
            highest = jnp.max(scores, -1, keepdims=True)
            weights = jnp.exp(scores - highest)
            total = jnp.sum(weights, -1, keepdims=True)
            mixed = jnp.dot(weights.astype(BF16), pairs, preferred_element_type=F32) / total
            level = highest + jnp.log(total)
            coarse = level.astype(BF16).astype(F32)
            medium = (level - coarse).astype(BF16).astype(F32)
            fine = level - coarse - medium
            parts = jnp.where(lane == 0, coarse, jnp.where(lane == 1, medium, fine))
            result = jnp.where(low, parts, mixed).astype(BF16)
            out[16 * chunk : 16 * chunk + 16, 16 * side : 16 * side + 16, :] = result.reshape(16, 16, 128)


def out_project_kernel(got, weight, out):
    total = None
    for head in range(3):
        sides = []
        for half in range(2):
            first = 8 * head + 4 * half
            block = got[first : first + 4].reshape(TOK, 128).astype(F32)
            level = block[:, 0:1] + block[:, 1:2] + block[:, 2:3]
            sides.append((block, level))
        (one, level_one), (two, level_two) = sides
        highest = jnp.maximum(level_one, level_two)
        share_one = jnp.exp(level_one - highest)
        share_two = jnp.exp(level_two - highest)
        mixed = (one * share_one + two * share_two) / (share_one + share_two)
        attended = mixed[:, 64:128].astype(BF16)
        term = jnp.dot(attended, weight[64 * head : 64 * head + 64, :], preferred_element_type=F32)
        total = term if total is None else total + term
    out[...] = total.astype(BF16).reshape(BLK, OWN, D)


def own_video(text):
    ids = index_of(SEQ_AXES) * TOK + index_of(BLK_AXES) * OWN + lax.broadcasted_iota(jnp.int32, (OWN, 1), 0)
    return ids >= text[0]


def sum_blocks(got):
    total = got[0].astype(F32)
    for block in range(1, got.shape[0]):
        total = total + got[block].astype(F32)
    return total


def after_attention_kernel(text, got, tokens, mods, weights, after, out, own, arrived):
    fetch = pltpu.make_async_copy(weights, own, arrived)
    fetch.start()
    pick = picker(mods, own_video(text))
    residual = tokens[0, pl.ds(pl.multiple_of(index_of(BLK_AXES) * OWN, OWN), OWN), :].astype(F32)
    summed = residual + pick(2) * sum_blocks(got)
    after[...] = summed
    normed = (layer_norm(summed, 1e-05) * (1.0 + pick(4)) + pick(3)).astype(BF16)
    for block in range(GROUP):
        out[block] = normed
    fetch.wait()


def feed_forward_kernel(rows, own, other, out):
    block = rows[...].reshape(GROUP * OWN, D)
    result = None
    for weights in (other, own):
        up = weights[:, 0:PIECE, :].reshape(D, UNITS)
        down = weights[:, PIECE : 2 * PIECE, :].reshape(D, UNITS)
        hidden = jnp.dot(block, up, preferred_element_type=F32)
        activated = jax.nn.gelu(hidden, approximate=True).astype(BF16)
        term = lax.dot_general(activated, down, ROWS_BY_ROWS, preferred_element_type=F32)
        result = term if result is None else result + term
    out[...] = result.astype(BF16).reshape(GROUP, OWN, D)


def pieces_kernel(up, down, out, arrived):
    copies = []
    for device in range(4):
        half = pl.ds(UNITS * (device % 2), UNITS)
        for side, weight in enumerate((up, down)):
            rows = pl.ds(PIECE * side, PIECE)
            copies.append(pltpu.make_async_copy(weight.at[:, half], out.at[device, rows, :], arrived.at[device, side]))
    for copy in copies:
        copy.start()
    for copy in copies:
        copy.wait()


def predict_kernel(text, got, after, mods, weight, hidden_out, predicted):
    pick = picker(mods, own_video(text))
    after_mlp = after[...] + pick(5) * sum_blocks(got)
    hidden_out[0] = after_mlp.astype(BF16)
    normed = (layer_norm(after_mlp, 1e-05) * (1.0 + pick(7)) + pick(6)).astype(BF16)
    predicted[...] = lax.dot_general(normed, weight[...], ROWS_BY_ROWS, preferred_element_type=F32)


def alpha_bar(last):
    row = lax.broadcasted_iota(jnp.int32, (8, 128), 0)
    steps = row * 128 + lax.broadcasted_iota(jnp.int32, (8, 128), 1)
    low, high = math.sqrt(0.00085), math.sqrt(0.012)
    root_beta = low + steps.astype(F32) / 999.0 * (high - low)
    kept = jnp.where(steps <= last, jnp.log1p(-jnp.where(steps < 1000, root_beta * root_beta, 0.0)), 0.0)
    return jnp.exp(jnp.sum(jnp.sum(kept, 1, keepdims=True), 0, keepdims=True))


def step_kernel(guidance, alphas, mine, other, latent, out):
    alpha_now, alpha_prev = alphas[0:1, 0:1], alphas[1:2, 0:1]
    is_cond = lax.axis_index("cfg") == 0
    own, partner = mine[...], other[...]
    cond = jnp.where(is_cond, own, partner)
    uncond = jnp.where(is_cond, partner, own)
    both = uncond + guidance[0] * (cond - uncond)
    guided = jnp.where(is_cond, both[:, 0:32], both[:, 32:64])
    held = latent[...]
    root_now, root_rest = jnp.sqrt(alpha_now), jnp.sqrt(1.0 - alpha_now)
    clean = root_now * held - root_rest * guided
    noise = root_rest * held + root_now * guided
    out[...] = jnp.sqrt(alpha_prev) * clean + jnp.sqrt(1.0 - alpha_prev) * noise


ALONE = 63


def call(kernel, specs, shapes, mib=24, scratch=()):
    return pl.pallas_call(
        kernel,
        out_shape=shapes,
        in_specs=specs,
        out_specs=jax.tree.map(lambda _: VMEM, shapes),
        scratch_shapes=scratch,
        compiler_params=pltpu.CompilerParams(vmem_limit_bytes=mib * 2**20),
        cost_estimate=pl.CostEstimate(flops=10_000_000, bytes_accessed=4_000_000, transcendentals=0),
    )


def body(
    tokens_in,
    modulation,
    qk_gain,
    qkv_weight,
    out_weight,
    up_weight,
    down_weight,
    proj_weight,
    latent,
    text_count,
    positions,
    step_index,
    guidance,
):
    pieces = call(
        pieces_kernel,
        [HBM, HBM],
        jax.ShapeDtypeStruct((4, 2 * PIECE, UNITS), BF16),
        mib=ALONE,
        scratch=[pltpu.SemaphoreType.DMA((4, 2))],
    )(up_weight, down_weight.T)
    pieces = lax.all_to_all(pieces, LINE, 0, 0, tiled=True)

    sent, alphas = call(
        project_kernel,
        [SMEM, SMEM] + [HBM] * 6,
        (jax.ShapeDtypeStruct((SEQ, 80, 128), BF16), jax.ShapeDtypeStruct((8, 128), F32)),
        mib=ALONE,
        scratch=[
            pltpu.VMEM((1, TOK, D), BF16),
            pltpu.VMEM((2, 8, D), F32),
            pltpu.VMEM((2, 64), F32),
            pltpu.VMEM((3, TOK), jnp.int32),
            pltpu.VMEM((8, 128), F32),
            pltpu.VMEM((3, 192, D), BF16),
            pltpu.SemaphoreType.DMA((6,)),
        ],
    )(text_count, step_index, tokens_in, modulation, qk_gain, positions, jnp.asarray(frequencies()), qkv_weight)
    sent, pieces = lax.optimization_barrier((sent, pieces))
    weights = lax.all_gather(pieces, "z", axis=0, tiled=True)
    got = lax.all_to_all(sent, SEQ_AXES, 0, 0, tiled=True)
    attended = call(attend_kernel, [VMEM], jax.ShapeDtypeStruct((SEQ, 32, 128), BF16))(got)
    back = lax.all_to_all(attended, SEQ_AXES, 0, 0, tiled=True)
    blocks = jax.ShapeDtypeStruct((BLK, OWN, D), BF16)
    shared = jax.ShapeDtypeStruct((GROUP, OWN, D), BF16)
    partial = call(out_project_kernel, [VMEM, VMEM], blocks)(back, out_weight)
    partial = lax.all_to_all(partial, BLK_AXES, 0, 0, tiled=True)
    partial, weights = lax.optimization_barrier((partial, weights))
    after, rows, own = call(
        after_attention_kernel,
        [SMEM, VMEM, VMEM, VMEM, HBM],
        (jax.ShapeDtypeStruct((OWN, D), F32), shared, jax.ShapeDtypeStruct((SEQ, 2 * PIECE, UNITS), BF16)),
        mib=50,
        scratch=[pltpu.SemaphoreType.DMA],
    )(text_count, partial, tokens_in, modulation, weights)
    rows = lax.all_to_all(rows, SHARERS, 0, 0, tiled=True)
    swapped = lax.ppermute(weights, "core", [(0, 1), (1, 0)])
    mlp = call(feed_forward_kernel, [VMEM, VMEM, VMEM], shared)(rows, own, swapped)
    mlp = lax.all_to_all(mlp, SHARERS, 0, 0, tiled=True)
    hidden_out, predicted = call(
        predict_kernel,
        [SMEM, VMEM, VMEM, VMEM, VMEM],
        (jax.ShapeDtypeStruct((1, OWN, D), BF16), jax.ShapeDtypeStruct((OWN, 64), F32)),
    )(text_count, mlp, after, modulation, proj_weight.T)
    partner = lax.ppermute(predicted, "cfg", [(0, 1), (1, 0)])
    latent_prev = call(
        step_kernel,
        [SMEM, VMEM, VMEM, VMEM, VMEM],
        jax.ShapeDtypeStruct((OWN, 32), F32),
    )(guidance, alphas, predicted, partner, latent)
    return (hidden_out, latent_prev)


def solution(mesh):
    devices = mesh.devices.reshape(2, 8, 2, 2, 4, 2)
    fine = jax.sharding.Mesh(devices, ("cfg", *SEQ_AXES, *BLK_AXES))
    rows = (*SEQ_AXES, *BLK_AXES)
    in_specs = (
        P("cfg", SEQ_AXES, None),
        P(),
        P(),
        P(None, BLK_AXES, None),
        P(BLK_AXES, None),
        P(SEQ_AXES, BLK_AXES),
        P(BLK_AXES, SEQ_AXES),
        P(),
        P(rows, "cfg"),
        P(),
        P(None, SEQ_AXES),
        P(),
        P(),
    )
    out_specs = (P("cfg", rows, None), P(rows, "cfg"))
    return jax.shard_map(body, mesh=fine, in_specs=in_specs, out_specs=out_specs, check_vma=False)
```

```python
import math

import jax
import jax.numpy as jnp
import numpy as np
from jax import lax
from jax.experimental import pallas as pl
from jax.experimental.pallas import tpu as pltpu
from jax.sharding import PartitionSpec as P

BF16 = jnp.bfloat16
F32 = jnp.float32
STRIDE = 20
TOK = 128
OWN = 16
D = 1536
UNITS = 384
SEQ = 32
BLK = 8
GROUP = 8
PIECE = 48

SEQ_AXES = ("z", "pair", "side")
LINE = ("pair", "side")
BLK_AXES = ("x", "core")
SHARERS = ("side", "x")

VMEM = pl.BlockSpec(memory_space=pltpu.VMEM)
SMEM = pl.BlockSpec(memory_space=pltpu.SMEM)
ANY = pl.BlockSpec(memory_space=pl.ANY)
HBM = pl.BlockSpec(memory_space=pltpu.HBM)

ROWS_BY_ROWS = (((1,), (1,)), ((), ()))


def frequencies():
    table = np.zeros((8, 128), np.float32)
    offset = 0
    for band, width in enumerate((16, 24, 24)):
        half = width // 2
        inverse = np.exp(-np.arange(half, dtype=np.float32) * np.float32(2.0 / width) * np.float32(math.log(10000.0)))
        for head in (0, 64):
            start = head + offset
            table[0, start : start + half] = inverse
            table[0, start + half : start + width] = inverse
            table[1, start : start + width] = band
            table[2, start : start + half] = 1.0
        offset += width
    return table


def index_of(axes):
    index = 0
    for axis in axes:
        index = index * lax.axis_size(axis) + lax.axis_index(axis)
    return index


def layer_norm(values, epsilon):
    centered = values - jnp.mean(values, -1, keepdims=True)
    spread = jnp.mean(centered * centered, -1, keepdims=True)
    return centered * lax.rsqrt(spread + epsilon)


def picker(mods, video):
    return lambda row: jnp.where(video, mods[1, row : row + 1, :], mods[0, row : row + 1, :])


def project_kernel(text, step, tokens_far, mods_far, gain_far, positions_far, table_far, qkv_far, out, alphas, *scratch):
    tokens, mods, gain, positions, table, qkv, arrived = scratch
    far = (tokens_far, mods_far, gain_far, positions_far, table_far, qkv_far)
    copies = [pltpu.make_async_copy(a, b, arrived.at[i]) for i, (a, b) in enumerate(zip(far, scratch))]
    for copy in copies:
        copy.start()
    row = lax.broadcasted_iota(jnp.int32, (8, 128), 0)
    alphas[...] = jnp.where(row == 0, alpha_bar(step[0]), alpha_bar(step[0] - STRIDE))
    for copy in copies[:5]:
        copy.wait()
    ids = index_of(SEQ_AXES) * TOK + lax.broadcasted_iota(jnp.int32, (TOK, 1), 0)
    video = ids >= text[0]
    pick = picker(mods, video)
    residual = tokens[0].astype(F32)
    normed = (layer_norm(residual, 1e-05) * (1.0 + pick(1)) + pick(0)).astype(BF16)

    def project(weight):
        return lax.dot_general(normed, weight, ROWS_BY_ROWS, preferred_element_type=F32)

    copies[5].wait()
    heads = project(qkv[0:2].reshape(384, D))
    values_low = project(qkv[2, 0:128, :])
    values_high = project(qkv[2, 64:192, :])

    lane = lax.broadcasted_iota(jnp.int32, (TOK, 128), 1)
    low = lane < 64
    band = table[1:2, :]
    where_at = positions[...].astype(F32)
    spread = [jnp.broadcast_to(where_at[a : a + 1, :], (128, 128)).T for a in range(3)]
    chosen = jnp.where(band == 0.0, spread[0], jnp.where(band == 1.0, spread[1], spread[2]))
    angles = chosen * table[0:1, :] * video.astype(F32)
    cosine = jnp.cos(angles)
    sine = jnp.sin(angles)
    first = table[2:3, :] > 0.5
    sine = jnp.where(first, -sine, sine)
    narrow = band == 0.0

    row_head = lax.broadcasted_iota(jnp.int32, (128, 128), 0) >> 6
    average = jnp.where(row_head == (lane >> 6), 1.0 / 64.0, 0.0)

    def head_mean(block):
        return jnp.dot(block, average, precision=lax.Precision.HIGHEST, preferred_element_type=F32)

    def prepare(block, gains):
        centered = block - head_mean(block)
        normal = centered * lax.rsqrt(head_mean(centered * centered) + 1e-06) * gains
        ahead = jnp.where(narrow, pltpu.roll(normal, 120, 1), pltpu.roll(normal, 116, 1))
        behind = jnp.where(narrow, pltpu.roll(normal, 8, 1), pltpu.roll(normal, 12, 1))
        return normal * cosine + jnp.where(first, ahead, behind) * sine

    query_gain = jnp.concatenate([gain[0:1, :], gain[0:1, :]], 1)
    key_gain = jnp.concatenate([gain[1:2, :], gain[1:2, :]], 1)
    mixed_gain = jnp.concatenate([gain[0:1, :], gain[1:2, :]], 1)
    queries_low = prepare(heads[:, 0:128], query_gain)
    query_and_key = prepare(heads[:, 128:256], mixed_gain)
    keys_high = prepare(heads[:, 256:384], key_gain)

    def turned(block):
        return pltpu.roll(block, 64, 1)

    pairs = [
        jnp.where(low, turned(query_and_key), turned(values_low)),
        jnp.where(low, keys_high, values_low),
        jnp.where(low, turned(keys_high), values_high),
    ]
    queries = [
        (queries_low, turned(queries_low)),
        (turned(queries_low), queries_low),
        (query_and_key, turned(query_and_key)),
    ]
    low16 = low[0:16, :]
    for head in range(3):
        pair = pairs[head].astype(BF16)
        left, right = queries[head]
        for part in range(4):
            start = 32 * part
            packed = jnp.where(low16, left[start : start + 16, :], right[start + 16 : start + 32, :])
            packed = (packed * 0.125).astype(BF16)
            for half in range(2):
                goes = 8 * head + 4 * half + part
                out[goes, 0:64, :] = pair[64 * half : 64 * half + 64, :]
                out[goes, 64:80, :] = packed
    out[24:32] = jnp.zeros((8, 80, 128), BF16)


def attend_kernel(got, out):
    pairs = got[:, 0:64, :].reshape(2048, 128)
    queries = got[:, 64:80, :].reshape(512, 128).astype(F32)
    lane = lax.broadcasted_iota(jnp.int32, (256, 128), 1)
    low = lane < 64
    for side in range(2):
        turned = queries if side == 0 else pltpu.roll(queries, 64, 1)
        for chunk in range(2):
            block = jnp.where(low, turned[256 * chunk : 256 * chunk + 256, :], 0.0).astype(BF16)
            scores = lax.dot_general(block, pairs, ROWS_BY_ROWS, preferred_element_type=F32)
            highest = jnp.max(scores, -1, keepdims=True)
            weights = jnp.exp(scores - highest)
            total = jnp.sum(weights, -1, keepdims=True)
            mixed = jnp.dot(weights.astype(BF16), pairs, preferred_element_type=F32) / total
            level = highest + jnp.log(total)
            coarse = level.astype(BF16).astype(F32)
            medium = (level - coarse).astype(BF16).astype(F32)
            fine = level - coarse - medium
            parts = jnp.where(lane == 0, coarse, jnp.where(lane == 1, medium, fine))
            result = jnp.where(low, parts, mixed).astype(BF16)
            out[16 * chunk : 16 * chunk + 16, 16 * side : 16 * side + 16, :] = result.reshape(16, 16, 128)


def out_project_kernel(got, weight, out):
    total = None
    for head in range(3):
        sides = []
        for half in range(2):
            first = 8 * head + 4 * half
            block = got[first : first + 4].reshape(TOK, 128).astype(F32)
            level = block[:, 0:1] + block[:, 1:2] + block[:, 2:3]
            sides.append((block, level))
        (one, level_one), (two, level_two) = sides
        highest = jnp.maximum(level_one, level_two)
        share_one = jnp.exp(level_one - highest)
        share_two = jnp.exp(level_two - highest)
        mixed = (one * share_one + two * share_two) / (share_one + share_two)
        attended = mixed[:, 64:128].astype(BF16)
        term = jnp.dot(attended, weight[64 * head : 64 * head + 64, :], preferred_element_type=F32)
        total = term if total is None else total + term
    out[...] = total.astype(BF16).reshape(BLK, OWN, D)


def own_video(text):
    ids = index_of(SEQ_AXES) * TOK + index_of(BLK_AXES) * OWN + lax.broadcasted_iota(jnp.int32, (OWN, 1), 0)
    return ids >= text[0]


def sum_blocks(got):
    total = got[0].astype(F32)
    for block in range(1, got.shape[0]):
        total = total + got[block].astype(F32)
    return total


def after_attention_kernel(text, got, tokens, mods, after, out):
    pick = picker(mods, own_video(text))
    residual = tokens[0, pl.ds(pl.multiple_of(index_of(BLK_AXES) * OWN, OWN), OWN), :].astype(F32)
    summed = residual + pick(2) * sum_blocks(got)
    after[...] = summed
    normed = (layer_norm(summed, 1e-05) * (1.0 + pick(4)) + pick(3)).astype(BF16)
    for block in range(GROUP):
        out[block] = normed


def feed_forward_kernel(rows, other, own_far, out, own, arrived):
    fetch = pltpu.make_async_copy(own_far, own, arrived)
    fetch.start()
    block = rows[...].reshape(GROUP * OWN, D)

    def term(weights):
        up = weights[:, 0:PIECE, :].reshape(D, UNITS)
        down = weights[:, PIECE : 2 * PIECE, :].reshape(D, UNITS)
        hidden = jnp.dot(block, up, preferred_element_type=F32)
        activated = jax.nn.gelu(hidden, approximate=True).astype(BF16)
        return lax.dot_general(activated, down, ROWS_BY_ROWS, preferred_element_type=F32)

    result = term(other)
    fetch.wait()
    out[...] = (result + term(own)).astype(BF16).reshape(GROUP, OWN, D)


def pieces_kernel(up, down, out, arrived):
    copies = []
    for device in range(4):
        half = pl.ds(UNITS * (device % 2), UNITS)
        for side, weight in enumerate((up, down)):
            rows = pl.ds(PIECE * side, PIECE)
            copies.append(pltpu.make_async_copy(weight.at[:, half], out.at[device, rows, :], arrived.at[device, side]))
    for copy in copies:
        copy.start()
    for copy in copies:
        copy.wait()


def predict_kernel(text, got, after, mods, weight, hidden_out, predicted):
    pick = picker(mods, own_video(text))
    after_mlp = after[...] + pick(5) * sum_blocks(got)
    hidden_out[0] = after_mlp.astype(BF16)
    normed = (layer_norm(after_mlp, 1e-05) * (1.0 + pick(7)) + pick(6)).astype(BF16)
    predicted[...] = lax.dot_general(normed, weight[...], ROWS_BY_ROWS, preferred_element_type=F32)


def alpha_bar(last):
    row = lax.broadcasted_iota(jnp.int32, (8, 128), 0)
    steps = row * 128 + lax.broadcasted_iota(jnp.int32, (8, 128), 1)
    low, high = math.sqrt(0.00085), math.sqrt(0.012)
    root_beta = low + steps.astype(F32) / 999.0 * (high - low)
    kept = jnp.where(steps <= last, jnp.log1p(-jnp.where(steps < 1000, root_beta * root_beta, 0.0)), 0.0)
    return jnp.exp(jnp.sum(jnp.sum(kept, 1, keepdims=True), 0, keepdims=True))


def step_kernel(guidance, alphas, mine, other, latent, out):
    alpha_now, alpha_prev = alphas[0:1, 0:1], alphas[1:2, 0:1]
    is_cond = lax.axis_index("cfg") == 0
    own, partner = mine[...], other[...]
    cond = jnp.where(is_cond, own, partner)
    uncond = jnp.where(is_cond, partner, own)
    both = uncond + guidance[0] * (cond - uncond)
    guided = jnp.where(is_cond, both[:, 0:32], both[:, 32:64])
    held = latent[...]
    root_now, root_rest = jnp.sqrt(alpha_now), jnp.sqrt(1.0 - alpha_now)
    clean = root_now * held - root_rest * guided
    noise = root_rest * held + root_now * guided
    out[...] = jnp.sqrt(alpha_prev) * clean + jnp.sqrt(1.0 - alpha_prev) * noise


ALONE = 63


def call(kernel, specs, shapes, mib=24, scratch=()):
    return pl.pallas_call(
        kernel,
        out_shape=shapes,
        in_specs=specs,
        out_specs=jax.tree.map(lambda _: VMEM, shapes),
        scratch_shapes=scratch,
        compiler_params=pltpu.CompilerParams(vmem_limit_bytes=mib * 2**20),
        cost_estimate=pl.CostEstimate(flops=10_000_000, bytes_accessed=4_000_000, transcendentals=0),
    )


def body(
    tokens_in,
    modulation,
    qk_gain,
    qkv_weight,
    out_weight,
    up_weight,
    down_weight,
    proj_weight,
    latent,
    text_count,
    positions,
    step_index,
    guidance,
):
    pieces = call(
        pieces_kernel,
        [HBM, HBM],
        jax.ShapeDtypeStruct((4, 2 * PIECE, UNITS), BF16),
        mib=ALONE,
        scratch=[pltpu.SemaphoreType.DMA((4, 2))],
    )(up_weight, down_weight.T)
    pieces = lax.all_to_all(pieces, LINE, 0, 0, tiled=True)

    sent, alphas = call(
        project_kernel,
        [SMEM, SMEM] + [HBM] * 6,
        (jax.ShapeDtypeStruct((SEQ, 80, 128), BF16), jax.ShapeDtypeStruct((8, 128), F32)),
        mib=ALONE,
        scratch=[
            pltpu.VMEM((1, TOK, D), BF16),
            pltpu.VMEM((2, 8, D), F32),
            pltpu.VMEM((2, 64), F32),
            pltpu.VMEM((3, TOK), jnp.int32),
            pltpu.VMEM((8, 128), F32),
            pltpu.VMEM((3, 192, D), BF16),
            pltpu.SemaphoreType.DMA((6,)),
        ],
    )(text_count, step_index, tokens_in, modulation, qk_gain, positions, jnp.asarray(frequencies()), qkv_weight)
    sent, pieces = lax.optimization_barrier((sent, pieces))
    weights = lax.all_gather(pieces, "z", axis=0, tiled=True)
    got = lax.all_to_all(sent, SEQ_AXES, 0, 0, tiled=True)
    attended = call(attend_kernel, [VMEM], jax.ShapeDtypeStruct((SEQ, 32, 128), BF16))(got)
    back = lax.all_to_all(attended, SEQ_AXES, 0, 0, tiled=True)
    blocks = jax.ShapeDtypeStruct((BLK, OWN, D), BF16)
    shared = jax.ShapeDtypeStruct((GROUP, OWN, D), BF16)
    partial = call(out_project_kernel, [VMEM, VMEM], blocks)(back, out_weight)
    partial = lax.all_to_all(partial, BLK_AXES, 0, 0, tiled=True)
    after, rows = call(
        after_attention_kernel,
        [SMEM, VMEM, VMEM, VMEM],
        (jax.ShapeDtypeStruct((OWN, D), F32), shared),
    )(text_count, partial, tokens_in, modulation)
    rows, weights = lax.optimization_barrier((rows, weights))
    rows = lax.all_to_all(rows, SHARERS, 0, 0, tiled=True)
    swapped = lax.ppermute(weights, "core", [(0, 1), (1, 0)])
    mlp = call(
        feed_forward_kernel,
        [VMEM, VMEM, HBM],
        shared,
        mib=50,
        scratch=[pltpu.VMEM((SEQ, 2 * PIECE, UNITS), BF16), pltpu.SemaphoreType.DMA],
    )(rows, swapped, weights)
    mlp = lax.all_to_all(mlp, SHARERS, 0, 0, tiled=True)
    hidden_out, predicted = call(
        predict_kernel,
        [SMEM, VMEM, VMEM, VMEM, VMEM],
        (jax.ShapeDtypeStruct((1, OWN, D), BF16), jax.ShapeDtypeStruct((OWN, 64), F32)),
    )(text_count, mlp, after, modulation, proj_weight.T)
    partner = lax.ppermute(predicted, "cfg", [(0, 1), (1, 0)])
    latent_prev = call(
        step_kernel,
        [SMEM, VMEM, VMEM, VMEM, VMEM],
        jax.ShapeDtypeStruct((OWN, 32), F32),
    )(guidance, alphas, predicted, partner, latent)
    return (hidden_out, latent_prev)


def solution(mesh):
    devices = mesh.devices.reshape(2, 8, 2, 2, 4, 2)
    fine = jax.sharding.Mesh(devices, ("cfg", *SEQ_AXES, *BLK_AXES))
    rows = (*SEQ_AXES, *BLK_AXES)
    in_specs = (
        P("cfg", SEQ_AXES, None),
        P(),
        P(),
        P(None, BLK_AXES, None),
        P(BLK_AXES, None),
        P(SEQ_AXES, BLK_AXES),
        P(BLK_AXES, SEQ_AXES),
        P(),
        P(rows, "cfg"),
        P(),
        P(None, SEQ_AXES),
        P(),
        P(),
    )
    out_specs = (P("cfg", rows, None), P(rows, "cfg"))
    return jax.shard_map(body, mesh=fine, in_specs=in_specs, out_specs=out_specs, check_vma=False)
```
